32 devices in a mesh: wide: 16 (over z, y, core), narrow: 2 (over x).
Axes of the slice: x: 2, y: 2, z: 4, core: 2. Of those that a mesh axis runs over, the one named last changes fastest.
Arguments:
- initial_warmth_state: float32 [128, 128, 256], P(None, 'wide', 'narrow'), may hold values from -1.5 to 1.5
- diffusivity_coefficient: float32 [128, 128, 256], P(None, 'wide', 'narrow'), may hold values from 0.5 to 8
- heating_supply: float32 [128, 128, 256], P(None, 'wide', 'narrow'), may hold values from -6 to 6
- known_forcing_vector: float32 [128, 128, 256], P(None, 'wide', 'narrow'), as said below
Outputs:
- advanced_warmth_state: float32 [128, 128, 256], P(None, 'wide', 'narrow')
- upcoming_forcing_vector: float32 [128, 128, 256], P(None, 'wide', 'narrow')
The draws below stay inside these ranges and needn't reach their ends.
Inputs may be any that keep to these rules, and one draw needn't show every extreme that they name: `known_forcing_vector`: values lie within -6 to 6.
All inputs are finite; a program needn't handle non-finite values.
Results may differ from the reference program's by a relative error of at most 0.00035.
Values sent between devices are 32-bit elements; how exact they have to be, the bound alone decides.
A program may use at most 64 MiB of HBM per device.

```python
import math
import jax
import jax.numpy as jnp

COUNT_ALONG_ONE = 128
COUNT_ALONG_TWO = 128
COUNT_ALONG_THREE = 256
HALF = 256


def draw_known_forcing_vector(key, part):
    grid_shape = (COUNT_ALONG_ONE, COUNT_ALONG_TWO, COUNT_ALONG_THREE)
    return jnp.clip(jax.random.normal(key, grid_shape, jnp.float32), -6.0, 6.0)


def steps_of(stream_key, dims, pieces, low, high):
    gain = 1.0
    for axis_at, parts in pieces:
        steps = jax.random.uniform(jax.random.fold_in(jax.random.fold_in(stream_key, 6), axis_at), (parts,), jnp.float32, low / len(pieces), high / len(pieces))
        gain = gain * jnp.repeat(jnp.exp(steps), dims[axis_at] // parts).reshape((-1,) + (1,) * (len(dims) - 1 - axis_at))
    return gain


def gaussian(rng, extent, width, bound, split=(), held_as=jnp.bfloat16):
    level = steps_of(rng, extent, split, -0.22, 0.18) if split else 1.0
    values = jax.random.normal(rng, extent, jnp.float32) * width * level
    return jnp.minimum(jnp.maximum(values, -bound), bound).astype(held_as)


def setup_inputs(seed: int = 0) -> dict:
    keys = jax.random.split(jax.random.key(seed), 5)
    initial_warmth_state = gaussian(keys[0], (COUNT_ALONG_ONE, COUNT_ALONG_TWO, COUNT_ALONG_THREE), 0.25, 1.5, ((1, 16), (2, 2)), jnp.float32)
    diffusivity_coefficient = jnp.clip(jnp.exp(math.log(8.0) - 2.7725887 * jax.random.uniform(keys[1], (COUNT_ALONG_ONE, COUNT_ALONG_TWO, COUNT_ALONG_THREE), jnp.float32) ** steps_of(keys[1], (COUNT_ALONG_ONE, COUNT_ALONG_TWO, COUNT_ALONG_THREE), ((1, 16), (2, 2)), -0.2, 0.2)), 0.5, 8.0)
    heating_supply = gaussian(keys[2], (COUNT_ALONG_ONE, COUNT_ALONG_TWO, COUNT_ALONG_THREE), 1.0, 6.0, ((1, 16), (2, 2)), jnp.float32)
    known_forcing_vector = draw_known_forcing_vector(jax.random.fold_in(keys[4], 71), 0)
    return {"initial_warmth_state": initial_warmth_state, "diffusivity_coefficient": diffusivity_coefficient, "heating_supply": heating_supply, "known_forcing_vector": known_forcing_vector}


def solve_lines(below_band, main_band, above_band, right_side):
    length = right_side.shape[0]
    if length == 1:
        return right_side / main_band
    blank = jnp.zeros_like(right_side[:1])
    if length % 2 == 1:
        solved = solve_lines(jnp.concatenate([below_band, blank]), jnp.concatenate([main_band, blank + 1.0]), jnp.concatenate([above_band, blank]), jnp.concatenate([right_side, blank]))
        return solved[:length]
    even_below = below_band[0::2]
    even_main = main_band[0::2]
    even_above = above_band[0::2]
    even_right = right_side[0::2]
    next_below = jnp.concatenate([even_below[1:], blank])
    next_main = jnp.concatenate([even_main[1:], blank + 1.0])
    next_above = jnp.concatenate([even_above[1:], blank])
    next_right = jnp.concatenate([even_right[1:], blank])
    factor_left = -below_band[1::2] / even_main
    factor_right = -above_band[1::2] / next_main
    reduced = solve_lines(factor_left * even_below, main_band[1::2] + factor_left * even_above + factor_right * next_below, factor_right * next_above, right_side[1::2] + factor_left * even_right + factor_right * next_right)
    earlier = jnp.concatenate([blank, reduced[:-1]])
    solved_even = (even_right - even_below * earlier - even_above * reduced) / even_main
    return jnp.stack([solved_even, reduced], axis=1).reshape(right_side.shape)


def line_solve(cond, right_side):
    half_ratio = 1.0 * HALF
    blank = jnp.zeros_like(cond[:1])
    padded = jnp.concatenate([blank, cond, blank])
    face_low = 0.5 * (padded[:-2] + padded[1:-1])
    face_high = 0.5 * (padded[1:-1] + padded[2:])
    below_band = jnp.concatenate([blank, -half_ratio * face_low[1:]])
    above_band = jnp.concatenate([-half_ratio * face_high[:-1], blank])
    main_band = 1.0 + half_ratio * (face_low + face_high)
    return solve_lines(below_band, main_band, above_band, right_side)


def operator(padded):
    field = padded[0]
    cond = padded[1]
    centre = field[1:-1, 1:-1, 1:-1]
    middle = cond[1:-1, 1:-1, 1:-1]
    total = 0.5 * (middle + cond[:-2, 1:-1, 1:-1]) * (field[:-2, 1:-1, 1:-1] - centre)
    total = total + 0.5 * (middle + cond[2:, 1:-1, 1:-1]) * (field[2:, 1:-1, 1:-1] - centre)
    total = total + 0.5 * (middle + cond[1:-1, :-2, 1:-1]) * (field[1:-1, :-2, 1:-1] - centre)
    total = total + 0.5 * (middle + cond[1:-1, 2:, 1:-1]) * (field[1:-1, 2:, 1:-1] - centre)
    total = total + 0.5 * (middle + cond[1:-1, 1:-1, :-2]) * (field[1:-1, 1:-1, :-2] - centre)
    total = total + 0.5 * (middle + cond[1:-1, 1:-1, 2:]) * (field[1:-1, 1:-1, 2:] - centre)
    return total


def reference(initial_warmth_state, diffusivity_coefficient, heating_supply, known_forcing_vector):
    time_ratio = 2.0 * HALF
    first = line_solve(diffusivity_coefficient, time_ratio * known_forcing_vector)
    second = jnp.swapaxes(line_solve(jnp.swapaxes(diffusivity_coefficient, 0, 1), jnp.swapaxes(first, 0, 1)), 0, 1)
    depthwise_pass = jnp.moveaxis(line_solve(jnp.moveaxis(diffusivity_coefficient, 2, 0), jnp.moveaxis(second, 2, 0)), 0, 2)
    advanced_warmth_state = initial_warmth_state + depthwise_pass
    joined_arrays = jnp.stack([advanced_warmth_state, diffusivity_coefficient])
    padded = jnp.pad(joined_arrays, ((0, 0), (1, 1), (1, 1), (1, 1)))
    upcoming_forcing_vector = heating_supply + operator(padded)
    return (advanced_warmth_state, upcoming_forcing_vector)
```

```python
import jax
import jax.numpy as jnp
from jax import lax
from jax.experimental import pallas as pl
from jax.experimental.pallas import tpu as pltpu
from jax.sharding import PartitionSpec as P

HALF = 256
HH = 0.5 * HALF
CELLS = 8
F32 = jnp.float32
MESH = pl.DeviceIdType.MESH


def factor(cs, lo, hi):
    n = len(cs)
    q, inv = [], []
    e = 1.0 + lo * cs[0]
    for i in range(n - 1):
        w = HH * (cs[i] + cs[i + 1])
        iv = 1.0 / (e + w)
        inv.append(iv)
        q.append(w * iv)
        e = 1.0 + q[i] * e
        if i == n - 2:
            e = e + hi * cs[n - 1]
    inv.append(1.0 / e)
    s = [None] * n
    s[1] = q[0]
    for i in range(2, n):
        s[i] = s[i - 1] * q[i - 1]
    first, last = [None] * n, [None] * n
    last[n - 1] = inv[n - 1]
    first[n - 1] = s[n - 1] * inv[n - 1]
    for i in range(n - 2, -1, -1):
        last[i] = q[i] * last[i + 1]
        first[i] = (inv[i] if i == 0 else s[i] * inv[i]) + q[i] * first[i + 1]
    return q, inv, first, last


def substitute(rs, q, inv):
    n = len(rs)
    s = [rs[0]]
    for i in range(1, n):
        s.append(rs[i] + q[i - 1] * s[i - 1])
    h = [None] * n
    h[n - 1] = s[n - 1] * inv[n - 1]
    for i in range(n - 2, -1, -1):
        h[i] = s[i] * inv[i] + q[i] * h[i + 1]
    return h


def chain_factor(diag, off):
    m, k = [], []
    for p in range(len(diag)):
        d = diag[p] if p == 0 else diag[p] - k[p - 1] * off[p - 1]
        m.append(1.0 / d)
        if p < len(off):
            k.append(m[p] * off[p])
    return m, k


def chain_solve(rhs, m, k):
    n = len(rhs)
    s = [rhs[0]]
    for p in range(1, n):
        s.append(rhs[p] + k[p - 1] * s[p - 1])
    f = [None] * n
    f[n - 1] = m[n - 1] * s[n - 1]
    for p in range(n - 2, -1, -1):
        f[p] = m[p] * s[p] + k[p] * f[p + 1]
    return f


def make_kernel(W, N, X, Y, Z):
    R = X // W
    XB, ZB = X // CELLS, Z // CELLS

    def row(ref, j):
        j = j * Y
        if not isinstance(j, int):
            j = pl.multiple_of(j, Y)
        return ref[pl.ds(j, Y), :]

    def put(ref, j, v):
        j = j * Y
        if not isinstance(j, int):
            j = pl.multiple_of(j, Y)
        ref[pl.ds(j, Y), :] = v

    def loop(count, body, unroll):
        def step(i, c):
            for u in range(unroll):
                body(i * unroll + u)
            return c
        lax.fori_loop(0, count // unroll, step, 0)

    def line_op(c_ref, v_ref, g, count, c_lo, v_lo, c_hi, v_hi):
        base = g * CELLS
        before = jnp.maximum(base - 1, 0)
        after = jnp.minimum(base + CELLS, count * CELLS - 1)
        cs = [row(c_ref, base + i) for i in range(CELLS)]
        vs = [row(v_ref, base + i) for i in range(CELLS)]
        cs = [jnp.where(g == 0, c_lo, row(c_ref, before))] + cs
        vs = [jnp.where(g == 0, v_lo, row(v_ref, before))] + vs
        cs.append(jnp.where(g == count - 1, c_hi, row(c_ref, after)))
        vs.append(jnp.where(g == count - 1, v_hi, row(v_ref, after)))
        fl = [0.5 * (cs[i] + cs[i + 1]) * (vs[i + 1] - vs[i]) for i in range(CELLS + 1)]
        return [fl[i + 1] - fl[i] for i in range(CELLS)]

    def kernel(init, cond, heat, known, adv, upc,
               hx, v1x, v8x, fx, first,
               cy, qy, iy, v1y, v8y, hy, sec,
               msend, mrecv, rsend, rrecv, sm, sk, fs, frecv,
               cz, iz, qz, nz_, v1z, v8z, hz, rz, fz, az, bz, mz, kz,
               zmat, zrhs, zf, lz, advy, chs, chr_, ahr,
               ms_s, ms_r, rs_s, rs_r, fs_s, fs_r, zm_s, zm_r, zr_s, zr_r, ch_s, ch_r, ah_s, ah_r):
        me = lax.axis_index("wide")
        mine = lax.axis_index("narrow")
        up = lax.rem(me + 1, W)
        down = lax.rem(me + W - 1, W)

        barrier = pltpu.get_barrier_semaphore()

        def greet(o, c):
            pl.semaphore_signal(barrier, inc=1, device_id={"wide": lax.rem(me + o, W)}, device_id_type=MESH)
            return c
        lax.fori_loop(1, W, greet, 0)
        for o in range(1, N):
            pl.semaphore_signal(barrier, inc=1, device_id={"narrow": lax.rem(mine + o, N)}, device_id_type=MESH)

        def remote(src, dst, ss, rs, **dev):
            return pltpu.make_async_remote_copy(
                src_ref=src, dst_ref=dst, send_sem=ss, recv_sem=rs, device_id=dev, device_id_type=MESH)

        lo_y = jnp.where(me == 0, HH, 0.0).astype(F32)
        hi_y = jnp.where(me == W - 1, HH, 0.0).astype(F32)

        def rows(s):
            return pl.ds(s * R, R)

        def strided(s, y):
            return pl.ds(s * (R * Y) + y, R, stride=Y)

        def y_matrix(s):
            cs = [cond[strided(s, y), :] for y in range(Y)]
            q, inv, a, b = factor(cs, lo_y, hi_y)
            for y in range(Y):
                cy[y, rows(s), :] = cs[y]
                if y < Y - 1:
                    qy[y, rows(s), :] = q[y]
                iy[y, rows(s), :] = inv[y]
                v1y[y, rows(s), :] = a[y]
                v8y[y, rows(s), :] = b[y]
        loop(W, y_matrix, 4)

        pl.semaphore_wait(barrier, W - 1 + N - 1)

        to_up = lambda src, dst, ss, rs: remote(src, dst.at[0], ss.at[0], rs.at[0], wide=up)
        to_down = lambda src, dst, ss, rs: remote(src, dst.at[1], ss.at[1], rs.at[1], wide=down)
        c_up = to_up(cy.at[Y - 1], chr_, ch_s, ch_r)
        c_down = to_down(cy.at[0], chr_, ch_s, ch_r)

        def start_pair(a, b):
            @pl.when(me < W - 1)
            def _():
                a.start()

            @pl.when(me > 0)
            def _():
                b.start()

        def recv_pair(a, b):
            @pl.when(me > 0)
            def _():
                a.wait_recv()

            @pl.when(me < W - 1)
            def _():
                b.wait_recv()

        def sent_pair(a, b):
            @pl.when(me < W - 1)
            def _():
                a.wait_send()

            @pl.when(me > 0)
            def _():
                b.wait_send()

        start_pair(c_up, c_down)

        def zero_ends(ref):
            @pl.when(me == 0)
            def _():
                ref[0] = jnp.zeros((X, Z), F32)

            @pl.when(me == W - 1)
            def _():
                ref[1] = jnp.zeros((X, Z), F32)
        zero_ends(chr_)
        zero_ends(ahr)

        def x_blocks(b):
            lo = jnp.where(b == 0, HH, 0.0).astype(F32)
            hi = jnp.where(b == XB - 1, HH, 0.0).astype(F32)
            cs = [row(cond, b * CELLS + i) for i in range(CELLS)]
            rs = [(2.0 * HALF) * row(known, b * CELLS + i) for i in range(CELLS)]
            q, inv, u, v = factor(cs, lo, hi)
            h = substitute(rs, q, inv)
            for i in range(CELLS):
                put(hx, b * CELLS + i, h[i])
                put(v1x, b * CELLS + i, u[i])
                put(v8x, b * CELLS + i, v[i])
        loop(XB, x_blocks, 4)

        recv_pair(c_up, c_down)

        def fill(s):
            w = HH * (chr_[0, rows(s), :] + cy[0, rows(s), :])
            msend[s, 0] = v1y[0, rows(s), :] + 1.0 / w
            msend[s, 1] = v8y[Y - 1, rows(s), :]
            msend[s, 2] = v8y[0, rows(s), :]
        loop(W, fill, 4)

        def exchange(send, recv, ss, rs, pick):
            def step(o, c):
                to = lax.rem(me + o, W)
                remote(pick(send, to), recv.at[me], ss.at[o], rs.at[o], wide=to).start()
                return c
            lax.fori_loop(1, W, step, 0)

        def arrived(send, recv, ss, rs, pick):
            def step(o, c):
                frm = lax.rem(me + W - o, W)
                remote(pick(send, frm), recv.at[frm], ss.at[o], rs.at[o], wide=frm).wait_recv()
                return c
            lax.fori_loop(1, W, step, 0)

        def left(send, recv, ss, rs, pick):
            def step(o, c):
                to = lax.rem(me + o, W)
                remote(pick(send, to), recv.at[me], ss.at[o], rs.at[o], wide=to).wait_send()
                return c
            lax.fori_loop(1, W, step, 0)

        one = lambda ref, s: ref.at[s]
        two = lambda ref, s: ref.at[pl.ds(s, 2)]
        exchange(msend, mrecv, ms_s, ms_r, one)
        mrecv[me] = msend[me]

        def inner(c_ref, a_ref, b_ref, blocks):
            diag, off = [], []
            for p in range(1, blocks):
                j = p * CELLS
                w = HH * (row(c_ref, j - 1) + row(c_ref, j))
                diag.append(1.0 / w + row(b_ref, j - 1) + row(a_ref, j))
                if p < blocks - 1:
                    off.append(row(b_ref, j))
            return chain_factor(diag, off)

        zero = jnp.zeros((Y, Z), F32)
        m, k = inner(cond, v1x, v8x, XB)
        f = chain_solve([row(hx, p * CELLS - 1) - row(hx, p * CELLS) for p in range(1, XB)], m, k)
        fx[0] = zero
        fx[XB] = zero
        for p in range(1, XB):
            fx[p] = f[p - 1]

        def x_final(b):
            fl, fr = fx[b], fx[b + 1]
            for i in range(CELLS):
                j = b * CELLS + i
                put(first, j, row(hx, j) + row(v1x, j) * fl - row(v8x, j) * fr)
        loop(XB, x_final, 4)

        def y_rhs(s):
            rs = [first[strided(s, y), :] for y in range(Y)]
            h = substitute(rs, [qy[y, rows(s), :] for y in range(Y - 1)], [iy[y, rows(s), :] for y in range(Y)])
            for y in range(Y):
                hy[y, rows(s), :] = h[y]
            rsend[s, 0] = h[0]
            rsend[s, 1] = h[Y - 1]
        loop(W, y_rhs, 4)
        exchange(rsend, rrecv, rs_s, rs_r, one)
        rrecv[me] = rsend[me]

        for y in range(Y):
            cz[pl.ds(y, Z, stride=Y), :] = cy[y].T
            iz[pl.ds(y, Z, stride=Y), :] = init[pl.ds(y, X, stride=Y), :].T
        lo_z = jnp.where(mine == 0, HH, 0.0).astype(F32)
        hi_z = jnp.where(mine == N - 1, HH, 0.0).astype(F32)

        def z_blocks(b):
            lo = jnp.where(b == 0, lo_z, 0.0)
            hi = jnp.where(b == ZB - 1, hi_z, 0.0)
            cs = [row(cz, b * CELLS + i) for i in range(CELLS)]
            q, inv, u, v = factor(cs, lo, hi)
            for i in range(CELLS):
                j = b * CELLS + i
                if i < CELLS - 1:
                    put(qz, j, q[i])
                put(nz_, j, inv[i])
                put(v1z, j, u[i])
                put(v8z, j, v[i])
        loop(ZB, z_blocks, 4)
        m, k = inner(cz, v1z, v8z, ZB)
        n = ZB - 1
        for p in range(n):
            mz[p] = m[p]
            if p < n - 1:
                kz[p] = k[p]
        g18_lo, g18_hi = row(v8z, 0), row(v8z, (ZB - 1) * CELLS)
        a = chain_solve([g18_lo] + [zero] * (n - 1), m, k)
        b = [None] * n
        b[n - 1] = m[n - 1] * g18_hi
        for p in range(n - 2, -1, -1):
            b[p] = k[p] * b[p + 1]
        for p in range(n):
            az[p + 1] = a[p]
            bz[p + 1] = b[p]
        one_plane = jnp.ones((Y, Z), F32)
        az[0], bz[0] = one_plane, zero
        az[ZB], bz[ZB] = zero, one_plane
        zmat[mine, 0] = row(v1z, 0) - g18_lo * a[0]
        zmat[mine, 1] = row(v8z, Z - 1) - g18_hi * b[n - 1]
        zmat[mine, 2] = g18_hi * a[n - 1]
        zmat[mine, 3] = row(cz, 0)
        zmat[mine, 4] = row(cz, Z - 1)
        zmat[mine, 5] = row(iz, 0)
        zmat[mine, 6] = row(iz, Z - 1)

        def z_copy(buf, ss, rs, o, who, slot):
            return remote(buf.at[slot], buf.at[slot], ss.at[o], rs.at[o], narrow=who)

        def z_send(buf, ss, rs):
            for o in range(1, N):
                z_copy(buf, ss, rs, o, lax.rem(mine + o, N), mine).start()

        def z_recv(buf, ss, rs):
            for o in range(1, N):
                frm = lax.rem(mine + N - o, N)
                z_copy(buf, ss, rs, o, frm, frm).wait_recv()

        def z_left(buf, ss, rs):
            for o in range(1, N):
                z_copy(buf, ss, rs, o, lax.rem(mine + o, N), mine).wait_send()
        z_send(zmat, zm_s, zm_r)

        arrived(msend, mrecv, ms_s, ms_r, one)
        m, k = chain_factor(
            [mrecv[p, 0] + mrecv[p - 1, 1] for p in range(1, W)], [mrecv[p, 2] for p in range(1, W - 1)])
        for p in range(W - 1):
            sm[p] = m[p]
            if p < W - 2:
                sk[p] = k[p]

        z_recv(zmat, zm_s, zm_r)
        below, above = jnp.maximum(mine - 1, 0), jnp.minimum(mine + 1, N - 1)
        has_lo = jnp.where(mine > 0, 1.0, 0.0).astype(F32)
        has_hi = jnp.where(mine < N - 1, 1.0, 0.0).astype(F32)
        z_c_lo, z_v_lo = has_lo * zmat[below, 4], has_lo * zmat[below, 6]
        z_c_hi, z_v_hi = has_hi * zmat[above, 3], has_hi * zmat[above, 5]

        def z_old(g):
            out = line_op(cz, iz, g, ZB, z_c_lo, z_v_lo, z_c_hi, z_v_hi)
            for i in range(CELLS):
                put(rz, g * CELLS + i, out[i])
        loop(ZB, z_old, 2)
        for y in range(Y):
            lz[y] = rz[pl.ds(y, Z, stride=Y), :].T

        arrived(rsend, rrecv, rs_s, rs_r, one)
        f = chain_solve(
            [rrecv[p - 1, 1] - rrecv[p, 0] for p in range(1, W)],
            [sm[p] for p in range(W - 1)], [sk[p] for p in range(W - 2)])
        edge = jnp.zeros((R, Z), F32)
        fs[0] = edge
        fs[W] = edge
        for p in range(1, W):
            fs[p] = f[p - 1]
        exchange(fs, frecv, fs_s, fs_r, two)
        frecv[me] = fs[pl.ds(me, 2)]
        arrived(fs, frecv, fs_s, fs_r, two)

        def y_final(s):
            fl, fr = frecv[s, 0], frecv[s, 1]
            for y in range(Y):
                sec[y, rows(s), :] = hy[y, rows(s), :] + v1y[y, rows(s), :] * fl - v8y[y, rows(s), :] * fr
        loop(W, y_final, 4)
        for y in range(Y):
            rz[pl.ds(y, Z, stride=Y), :] = sec[y].T

        def z_rhs(b):
            j = b * CELLS
            h = substitute([row(rz, j + i) for i in range(CELLS)], [row(qz, j + i) for i in range(CELLS - 1)],
                           [row(nz_, j + i) for i in range(CELLS)])
            for i in range(CELLS):
                put(hz, j + i, h[i])
        loop(ZB, z_rhs, 4)
        f = chain_solve([row(hz, p * CELLS - 1) - row(hz, p * CELLS) for p in range(1, ZB)],
                        [mz[p] for p in range(n)], [kz[p] for p in range(n - 1)])
        for p in range(n):
            fz[p + 1] = f[p]
        fz[0] = zero
        fz[ZB] = zero
        zrhs[mine, 0] = row(hz, 0) - row(v8z, 0) * f[0]
        zrhs[mine, 1] = row(hz, Z - 1) + row(v8z, (ZB - 1) * CELLS) * f[n - 1]
        z_send(zrhs, zr_s, zr_r)
        m, k = chain_factor(
            [1.0 / (HH * (zmat[p - 1, 4] + zmat[p, 3])) + zmat[p - 1, 1] + zmat[p, 0] for p in range(1, N)],
            [zmat[p, 2] for p in range(1, N - 1)])
        z_recv(zrhs, zr_s, zr_r)
        f = chain_solve([zrhs[p - 1, 1] - zrhs[p, 0] for p in range(1, N)], m, k)
        zf[0] = zero
        zf[N] = zero
        for p in range(1, N):
            zf[p] = f[p - 1]
        z_fl, z_fr = zf[mine], zf[mine + 1]

        def z_final(b):
            fl = fz[b] + az[b] * z_fl + bz[b] * z_fr
            fr = fz[b + 1] + az[b + 1] * z_fl + bz[b + 1] * z_fr
            for i in range(CELLS):
                j = b * CELLS + i
                put(rz, j, row(hz, j) + row(v1z, j) * fl - row(v8z, j) * fr)
        loop(ZB, z_final, 4)

        a_up = to_up(advy.at[Y - 1], ahr, ah_s, ah_r)
        a_down = to_down(advy.at[0], ahr, ah_s, ah_r)

        def new_state(y):
            third = rz[pl.ds(y, Z, stride=Y), :].T
            state = init[pl.ds(y, X, stride=Y), :] + third
            advy[y] = state
            lz[y] = lz[y] + (third - sec[y]) * (1.0 / HALF)
            adv[pl.ds(y, X, stride=Y), :] = state
        new_state(0)
        new_state(Y - 1)
        start_pair(a_up, a_down)
        for y in range(1, Y - 1):
            new_state(y)

        def y_op(s):
            cs = [cy[y, rows(s), :] for y in range(Y)]
            vs = [advy[y, rows(s), :] for y in range(Y)]
            fl = [0.5 * (cs[i] + cs[i + 1]) * (vs[i + 1] - vs[i]) for i in range(Y - 1)]
            for y in range(Y):
                out = lz[y, rows(s), :]
                if y < Y - 1:
                    out = out + fl[y]
                if y > 0:
                    out = out - fl[y - 1]
                upc[strided(s, y), :] = out
        loop(W, y_op, 4)

        def x_op(g):
            out = line_op(cond, adv, g, XB, zero, zero, zero, zero)
            for i in range(CELLS):
                j = g * CELLS + i
                put(upc, j, row(upc, j) + (row(heat, j) + out[i]))
        loop(XB, x_op, 2)

        recv_pair(a_up, a_down)

        def y_ends(s):
            for slot, y in ((0, 0), (1, Y - 1)):
                fl = 0.5 * (chr_[slot, rows(s), :] + cy[y, rows(s), :]) * (ahr[slot, rows(s), :] - advy[y, rows(s), :])
                upc[strided(s, y), :] = upc[strided(s, y), :] + fl
        loop(W, y_ends, 4)

        sent_pair(c_up, c_down)
        sent_pair(a_up, a_down)
        left(msend, mrecv, ms_s, ms_r, one)
        left(rsend, rrecv, rs_s, rs_r, one)
        left(fs, frecv, fs_s, fs_r, two)
        z_left(zmat, zm_s, zm_r)
        z_left(zrhs, zr_s, zr_r)

    flat = pltpu.VMEM((X * Y, Z), F32)
    planes = pltpu.VMEM((Y, X, Z), F32)
    flux = lambda count: pltpu.VMEM((count, Y, Z), F32)
    part = lambda *lead: pltpu.VMEM((*lead, R, Z), F32)
    sems = lambda count: pltpu.SemaphoreType.DMA((count,))
    scratch = [flat, flat, flat, flux(XB + 1), flat,
               planes, planes, planes, planes, planes, planes, planes,
               part(W, 3), part(W, 3), part(W, 2), part(W, 2), part(W), part(W), part(W + 1), part(W, 2),
               flat, flat, flat, flat, flat, flat, flat, flat,
               flux(ZB + 1), flux(ZB + 1), flux(ZB + 1), flux(ZB), flux(ZB),
               pltpu.VMEM((N, 7, Y, Z), F32), pltpu.VMEM((N, 2, Y, Z), F32), flux(N + 1), planes, planes,
               pltpu.VMEM((8, Z), F32), pltpu.VMEM((2, X, Z), F32), pltpu.VMEM((2, X, Z), F32),
               sems(W), sems(W), sems(W), sems(W), sems(W), sems(W), sems(N), sems(N), sems(N), sems(N),
               sems(2), sems(2), sems(2), sems(2)]
    return kernel, scratch


def solution(mesh):
    W, N = mesh.shape["wide"], mesh.shape["narrow"]

    def per_device(*arrays):
        X, Y, Z = arrays[0].shape
        kernel, scratch = make_kernel(W, N, X, Y, Z)
        vmem = pl.BlockSpec(memory_space=pltpu.VMEM)
        out = jax.ShapeDtypeStruct((X * Y, Z), F32)
        results = pl.pallas_call(
            kernel,
            out_shape=(out, out),
            in_specs=[vmem] * 4,
            out_specs=(vmem, vmem),
            scratch_shapes=scratch,
            compiler_params=pltpu.CompilerParams(
                collective_id=0, has_side_effects=True, vmem_limit_bytes=48 * 1024 * 1024),
        )(*[a.reshape(X * Y, Z) for a in arrays])
        return tuple(r.reshape(X, Y, Z) for r in results)

    placed = P(None, "wide", "narrow")
    return jax.shard_map(
        per_device, mesh=mesh, in_specs=(placed,) * 4, out_specs=(placed, placed), check_vma=False)
```

```python
import jax
import jax.numpy as jnp
from jax import lax
from jax.experimental import pallas as pl
from jax.experimental.pallas import tpu as pltpu
from jax.sharding import PartitionSpec as P

HALF = 256
HH = 0.5 * HALF
CELLS = 8
F32 = jnp.float32
MESH = pl.DeviceIdType.MESH


def factor(cs, lo, hi):
    n = len(cs)
    q, inv = [], []
    e = 1.0 + lo * cs[0]
    for i in range(n - 1):
        w = HH * (cs[i] + cs[i + 1])
        iv = 1.0 / (e + w)
        inv.append(iv)
        q.append(w * iv)
        e = 1.0 + q[i] * e
        if i == n - 2:
            e = e + hi * cs[n - 1]
    inv.append(1.0 / e)
    s = [None] * n
    s[1] = q[0]
    for i in range(2, n):
        s[i] = s[i - 1] * q[i - 1]
    first, last = [None] * n, [None] * n
    last[n - 1] = inv[n - 1]
    first[n - 1] = s[n - 1] * inv[n - 1]
    for i in range(n - 2, -1, -1):
        last[i] = q[i] * last[i + 1]
        first[i] = (inv[i] if i == 0 else s[i] * inv[i]) + q[i] * first[i + 1]
    return q, inv, first, last


def substitute(rs, q, inv):
    n = len(rs)
    s = [rs[0]]
    for i in range(1, n):
        s.append(rs[i] + q[i - 1] * s[i - 1])
    h = [None] * n
    h[n - 1] = s[n - 1] * inv[n - 1]
    for i in range(n - 2, -1, -1):
        h[i] = s[i] * inv[i] + q[i] * h[i + 1]
    return h


def chain_factor(diag, off):
    m, k = [], []
    for p in range(len(diag)):
        d = diag[p] if p == 0 else diag[p] - k[p - 1] * off[p - 1]
        m.append(1.0 / d)
        if p < len(off):
            k.append(m[p] * off[p])
    return m, k


def chain_solve(rhs, m, k):
    n = len(rhs)
    s = [rhs[0]]
    for p in range(1, n):
        s.append(rhs[p] + k[p - 1] * s[p - 1])
    f = [None] * n
    f[n - 1] = m[n - 1] * s[n - 1]
    for p in range(n - 2, -1, -1):
        f[p] = m[p] * s[p] + k[p] * f[p + 1]
    return f


def make_kernel(W, N, X, Y, Z):
    R = X // W
    XB, ZB = X // CELLS, Z // CELLS

    def row(ref, j):
        j = j * Y
        if not isinstance(j, int):
            j = pl.multiple_of(j, Y)
        return ref[pl.ds(j, Y), :]

    def put(ref, j, v):
        j = j * Y
        if not isinstance(j, int):
            j = pl.multiple_of(j, Y)
        ref[pl.ds(j, Y), :] = v

    def loop(count, body, unroll):
        def step(i, c):
            for u in range(unroll):
                body(i * unroll + u)
            return c
        lax.fori_loop(0, count // unroll, step, 0)

    def line_op(c_ref, v_ref, g, count, c_lo, v_lo, c_hi, v_hi):
        base = g * CELLS
        before = jnp.maximum(base - 1, 0)
        after = jnp.minimum(base + CELLS, count * CELLS - 1)
        cs = [row(c_ref, base + i) for i in range(CELLS)]
        vs = [row(v_ref, base + i) for i in range(CELLS)]
        cs = [jnp.where(g == 0, c_lo, row(c_ref, before))] + cs
        vs = [jnp.where(g == 0, v_lo, row(v_ref, before))] + vs
        cs.append(jnp.where(g == count - 1, c_hi, row(c_ref, after)))
        vs.append(jnp.where(g == count - 1, v_hi, row(v_ref, after)))
        fl = [0.5 * (cs[i] + cs[i + 1]) * (vs[i + 1] - vs[i]) for i in range(CELLS + 1)]
        return [fl[i + 1] - fl[i] for i in range(CELLS)]

    def kernel(init_h, cond_h, heat_h, known_h, adv, upc,
               init, cond, heat, known,
               hx, v1x, v8x, fx, first,
               cy, qy, iy, v1y, v8y, hy, sec,
               msend, mrecv, rsend, rrecv, sm, sk, fs, frecv,
               cz, iz, qz, nz_, v1z, v8z, hz, rz, fz, az, bz, mz, kz,
               zmat, zrhs, zf, lz, advy, chs, chr_, ahr,
               ms_s, ms_r, rs_s, rs_r, fs_s, fs_r, zm_s, zm_r, zr_s, zr_r, ch_s, ch_r, ah_s, ah_r, in_s):
        me = lax.axis_index("wide")
        mine = lax.axis_index("narrow")
        up = lax.rem(me + 1, W)
        down = lax.rem(me + W - 1, W)

        barrier = pltpu.get_barrier_semaphore()

        def greet(o, c):
            pl.semaphore_signal(barrier, inc=1, device_id={"wide": lax.rem(me + o, W)}, device_id_type=MESH)
            return c
        lax.fori_loop(1, W, greet, 0)
        for o in range(1, N):
            pl.semaphore_signal(barrier, inc=1, device_id={"narrow": lax.rem(mine + o, N)}, device_id_type=MESH)

        loads = [pltpu.make_async_copy(a, b, in_s.at[i]) for i, (a, b) in enumerate(
            ((cond_h, cond), (known_h, known), (init_h, init), (heat_h, heat)))]
        for load in loads:
            load.start()

        def remote(src, dst, ss, rs, **dev):
            return pltpu.make_async_remote_copy(
                src_ref=src, dst_ref=dst, send_sem=ss, recv_sem=rs, device_id=dev, device_id_type=MESH)

        lo_y = jnp.where(me == 0, HH, 0.0).astype(F32)
        hi_y = jnp.where(me == W - 1, HH, 0.0).astype(F32)

        def rows(s):
            return pl.ds(s * R, R)

        def strided(s, y):
            return pl.ds(s * (R * Y) + y, R, stride=Y)

        loads[0].wait()

        def y_matrix(s):
            cs = [cond[strided(s, y), :] for y in range(Y)]
            q, inv, a, b = factor(cs, lo_y, hi_y)
            for y in range(Y):
                cy[y, rows(s), :] = cs[y]
                if y < Y - 1:
                    qy[y, rows(s), :] = q[y]
                iy[y, rows(s), :] = inv[y]
                v1y[y, rows(s), :] = a[y]
                v8y[y, rows(s), :] = b[y]
        loop(W, y_matrix, 4)

        to_up = lambda src, dst, ss, rs: remote(src, dst.at[0], ss.at[0], rs.at[0], wide=up)
        to_down = lambda src, dst, ss, rs: remote(src, dst.at[1], ss.at[1], rs.at[1], wide=down)
        c_up = to_up(cy.at[Y - 1], chr_, ch_s, ch_r)
        c_down = to_down(cy.at[0], chr_, ch_s, ch_r)

        def start_pair(a, b):
            @pl.when(me < W - 1)
            def _():
                a.start()

            @pl.when(me > 0)
            def _():
                b.start()

        def recv_pair(a, b):
            @pl.when(me > 0)
            def _():
                a.wait_recv()

            @pl.when(me < W - 1)
            def _():
                b.wait_recv()

        def sent_pair(a, b):
            @pl.when(me < W - 1)
            def _():
                a.wait_send()

            @pl.when(me > 0)
            def _():
                b.wait_send()

        def zero_ends(ref):
            @pl.when(me == 0)
            def _():
                ref[0] = jnp.zeros((X, Z), F32)

            @pl.when(me == W - 1)
            def _():
                ref[1] = jnp.zeros((X, Z), F32)
        zero_ends(chr_)
        zero_ends(ahr)

        loads[1].wait()
        def x_blocks(b):
            lo = jnp.where(b == 0, HH, 0.0).astype(F32)
            hi = jnp.where(b == XB - 1, HH, 0.0).astype(F32)
            cs = [row(cond, b * CELLS + i) for i in range(CELLS)]
            rs = [(2.0 * HALF) * row(known, b * CELLS + i) for i in range(CELLS)]
            q, inv, u, v = factor(cs, lo, hi)
            h = substitute(rs, q, inv)
            for i in range(CELLS):
                put(hx, b * CELLS + i, h[i])
                put(v1x, b * CELLS + i, u[i])
                put(v8x, b * CELLS + i, v[i])
        loop(XB, x_blocks, 4)

        def exchange(send, recv, ss, rs, pick):
            def step(o, c):
                to = lax.rem(me + o, W)
                remote(pick(send, to), recv.at[me], ss.at[o], rs.at[o], wide=to).start()
                return c
            lax.fori_loop(1, W, step, 0)

        def arrived(send, recv, ss, rs, pick):
            def step(o, c):
                frm = lax.rem(me + W - o, W)
                remote(pick(send, frm), recv.at[frm], ss.at[o], rs.at[o], wide=frm).wait_recv()
                return c
            lax.fori_loop(1, W, step, 0)

        def left(send, recv, ss, rs, pick):
            def step(o, c):
                to = lax.rem(me + o, W)
                remote(pick(send, to), recv.at[me], ss.at[o], rs.at[o], wide=to).wait_send()
                return c
            lax.fori_loop(1, W, step, 0)

        one = lambda ref, s: ref.at[s]
        two = lambda ref, s: ref.at[pl.ds(s, 2)]
        def inner(c_ref, a_ref, b_ref, blocks):
            diag, off = [], []
            for p in range(1, blocks):
                j = p * CELLS
                w = HH * (row(c_ref, j - 1) + row(c_ref, j))
                diag.append(1.0 / w + row(b_ref, j - 1) + row(a_ref, j))
                if p < blocks - 1:
                    off.append(row(b_ref, j))
            return chain_factor(diag, off)

        zero = jnp.zeros((Y, Z), F32)
        m, k = inner(cond, v1x, v8x, XB)
        f = chain_solve([row(hx, p * CELLS - 1) - row(hx, p * CELLS) for p in range(1, XB)], m, k)
        fx[0] = zero
        fx[XB] = zero
        for p in range(1, XB):
            fx[p] = f[p - 1]

        def x_final(b):
            fl, fr = fx[b], fx[b + 1]
            for i in range(CELLS):
                j = b * CELLS + i
                put(first, j, row(hx, j) + row(v1x, j) * fl - row(v8x, j) * fr)
        loop(XB, x_final, 4)

        def y_rhs(s):
            rs = [first[strided(s, y), :] for y in range(Y)]
            h = substitute(rs, [qy[y, rows(s), :] for y in range(Y - 1)], [iy[y, rows(s), :] for y in range(Y)])
            for y in range(Y):
                hy[y, rows(s), :] = h[y]
            rsend[s, 0] = h[0]
            rsend[s, 1] = h[Y - 1]
        loop(W, y_rhs, 4)
        pl.semaphore_wait(barrier, W - 1 + N - 1)
        start_pair(c_up, c_down)
        exchange(rsend, rrecv, rs_s, rs_r, one)
        rrecv[me] = rsend[me]

        recv_pair(c_up, c_down)

        def fill(s):
            w = HH * (chr_[0, rows(s), :] + cy[0, rows(s), :])
            msend[s, 0] = v1y[0, rows(s), :] + 1.0 / w
            msend[s, 1] = v8y[Y - 1, rows(s), :]
            msend[s, 2] = v8y[0, rows(s), :]
        loop(W, fill, 4)

        exchange(msend, mrecv, ms_s, ms_r, one)
        mrecv[me] = msend[me]

        loads[2].wait()
        for y in range(Y):
            cz[pl.ds(y, Z, stride=Y), :] = cy[y].T
            iz[pl.ds(y, Z, stride=Y), :] = init[pl.ds(y, X, stride=Y), :].T
        lo_z = jnp.where(mine == 0, HH, 0.0).astype(F32)
        hi_z = jnp.where(mine == N - 1, HH, 0.0).astype(F32)

        def z_blocks(b):
            lo = jnp.where(b == 0, lo_z, 0.0)
            hi = jnp.where(b == ZB - 1, hi_z, 0.0)
            cs = [row(cz, b * CELLS + i) for i in range(CELLS)]
            q, inv, u, v = factor(cs, lo, hi)
            for i in range(CELLS):
                j = b * CELLS + i
                if i < CELLS - 1:
                    put(qz, j, q[i])
                put(nz_, j, inv[i])
                put(v1z, j, u[i])
                put(v8z, j, v[i])
        loop(ZB, z_blocks, 4)
        m, k = inner(cz, v1z, v8z, ZB)
        n = ZB - 1
        for p in range(n):
            mz[p] = m[p]
            if p < n - 1:
                kz[p] = k[p]
        g18_lo, g18_hi = row(v8z, 0), row(v8z, (ZB - 1) * CELLS)
        a = chain_solve([g18_lo] + [zero] * (n - 1), m, k)
        b = [None] * n
        b[n - 1] = m[n - 1] * g18_hi
        for p in range(n - 2, -1, -1):
            b[p] = k[p] * b[p + 1]
        for p in range(n):
            az[p + 1] = a[p]
            bz[p + 1] = b[p]
        one_plane = jnp.ones((Y, Z), F32)
        az[0], bz[0] = one_plane, zero
        az[ZB], bz[ZB] = zero, one_plane
        zmat[mine, 0] = row(v1z, 0) - g18_lo * a[0]
        zmat[mine, 1] = row(v8z, Z - 1) - g18_hi * b[n - 1]
        zmat[mine, 2] = g18_hi * a[n - 1]
        zmat[mine, 3] = row(cz, 0)
        zmat[mine, 4] = row(cz, Z - 1)
        zmat[mine, 5] = row(iz, 0)
        zmat[mine, 6] = row(iz, Z - 1)

        def z_copy(buf, ss, rs, o, who, slot):
            return remote(buf.at[slot], buf.at[slot], ss.at[o], rs.at[o], narrow=who)

        def z_send(buf, ss, rs):
            for o in range(1, N):
                z_copy(buf, ss, rs, o, lax.rem(mine + o, N), mine).start()

        def z_recv(buf, ss, rs):
            for o in range(1, N):
                frm = lax.rem(mine + N - o, N)
                z_copy(buf, ss, rs, o, frm, frm).wait_recv()

        def z_left(buf, ss, rs):
            for o in range(1, N):
                z_copy(buf, ss, rs, o, lax.rem(mine + o, N), mine).wait_send()
        z_send(zmat, zm_s, zm_r)

        arrived(msend, mrecv, ms_s, ms_r, one)
        m, k = chain_factor(
            [mrecv[p, 0] + mrecv[p - 1, 1] for p in range(1, W)], [mrecv[p, 2] for p in range(1, W - 1)])
        for p in range(W - 1):
            sm[p] = m[p]
            if p < W - 2:
                sk[p] = k[p]

        z_recv(zmat, zm_s, zm_r)
        below, above = jnp.maximum(mine - 1, 0), jnp.minimum(mine + 1, N - 1)
        has_lo = jnp.where(mine > 0, 1.0, 0.0).astype(F32)
        has_hi = jnp.where(mine < N - 1, 1.0, 0.0).astype(F32)
        z_c_lo, z_v_lo = has_lo * zmat[below, 4], has_lo * zmat[below, 6]
        z_c_hi, z_v_hi = has_hi * zmat[above, 3], has_hi * zmat[above, 5]

        def z_old(g):
            out = line_op(cz, iz, g, ZB, z_c_lo, z_v_lo, z_c_hi, z_v_hi)
            for i in range(CELLS):
                put(rz, g * CELLS + i, out[i])
        loop(ZB, z_old, 2)
        for y in range(Y):
            lz[y] = rz[pl.ds(y, Z, stride=Y), :].T

        arrived(rsend, rrecv, rs_s, rs_r, one)
        f = chain_solve(
            [rrecv[p - 1, 1] - rrecv[p, 0] for p in range(1, W)],
            [sm[p] for p in range(W - 1)], [sk[p] for p in range(W - 2)])
        edge = jnp.zeros((R, Z), F32)
        fs[0] = edge
        fs[W] = edge
        for p in range(1, W):
            fs[p] = f[p - 1]
        exchange(fs, frecv, fs_s, fs_r, two)
        frecv[me] = fs[pl.ds(me, 2)]
        arrived(fs, frecv, fs_s, fs_r, two)

        def y_final(s):
            fl, fr = frecv[s, 0], frecv[s, 1]
            for y in range(Y):
                sec[y, rows(s), :] = hy[y, rows(s), :] + v1y[y, rows(s), :] * fl - v8y[y, rows(s), :] * fr
        loop(W, y_final, 4)
        for y in range(Y):
            rz[pl.ds(y, Z, stride=Y), :] = sec[y].T

        def z_rhs(b):
            j = b * CELLS
            h = substitute([row(rz, j + i) for i in range(CELLS)], [row(qz, j + i) for i in range(CELLS - 1)],
                           [row(nz_, j + i) for i in range(CELLS)])
            for i in range(CELLS):
                put(hz, j + i, h[i])
        loop(ZB, z_rhs, 4)
        f = chain_solve([row(hz, p * CELLS - 1) - row(hz, p * CELLS) for p in range(1, ZB)],
                        [mz[p] for p in range(n)], [kz[p] for p in range(n - 1)])
        for p in range(n):
            fz[p + 1] = f[p]
        fz[0] = zero
        fz[ZB] = zero
        zrhs[mine, 0] = row(hz, 0) - row(v8z, 0) * f[0]
        zrhs[mine, 1] = row(hz, Z - 1) + row(v8z, (ZB - 1) * CELLS) * f[n - 1]
        z_send(zrhs, zr_s, zr_r)
        m, k = chain_factor(
            [1.0 / (HH * (zmat[p - 1, 4] + zmat[p, 3])) + zmat[p - 1, 1] + zmat[p, 0] for p in range(1, N)],
            [zmat[p, 2] for p in range(1, N - 1)])
        z_recv(zrhs, zr_s, zr_r)
        f = chain_solve([zrhs[p - 1, 1] - zrhs[p, 0] for p in range(1, N)], m, k)
        zf[0] = zero
        zf[N] = zero
        for p in range(1, N):
            zf[p] = f[p - 1]
        z_fl, z_fr = zf[mine], zf[mine + 1]

        def z_final(b):
            fl = fz[b] + az[b] * z_fl + bz[b] * z_fr
            fr = fz[b + 1] + az[b + 1] * z_fl + bz[b + 1] * z_fr
            for i in range(CELLS):
                j = b * CELLS + i
                put(rz, j, row(hz, j) + row(v1z, j) * fl - row(v8z, j) * fr)
        loop(ZB, z_final, 4)

        a_up = to_up(advy.at[Y - 1], ahr, ah_s, ah_r)
        a_down = to_down(advy.at[0], ahr, ah_s, ah_r)

        def new_state(y):
            third = rz[pl.ds(y, Z, stride=Y), :].T
            state = init[pl.ds(y, X, stride=Y), :] + third
            advy[y] = state
            lz[y] = lz[y] + (third - sec[y]) * (1.0 / HALF)
            adv[pl.ds(y, X, stride=Y), :] = state
        new_state(0)
        new_state(Y - 1)
        start_pair(a_up, a_down)
        for y in range(1, Y - 1):
            new_state(y)

        def y_op(s):
            cs = [cy[y, rows(s), :] for y in range(Y)]
            vs = [advy[y, rows(s), :] for y in range(Y)]
            fl = [0.5 * (cs[i] + cs[i + 1]) * (vs[i + 1] - vs[i]) for i in range(Y - 1)]
            for y in range(Y):
                out = lz[y, rows(s), :]
                if y < Y - 1:
                    out = out + fl[y]
                if y > 0:
                    out = out - fl[y - 1]
                upc[strided(s, y), :] = out
        loop(W, y_op, 4)

        loads[3].wait()

        def x_op(g):
            out = line_op(cond, adv, g, XB, zero, zero, zero, zero)
            for i in range(CELLS):
                j = g * CELLS + i
                put(upc, j, row(upc, j) + (row(heat, j) + out[i]))
        loop(XB, x_op, 2)

        recv_pair(a_up, a_down)

        def y_ends(s):
            for slot, y in ((0, 0), (1, Y - 1)):
                fl = 0.5 * (chr_[slot, rows(s), :] + cy[y, rows(s), :]) * (ahr[slot, rows(s), :] - advy[y, rows(s), :])
                upc[strided(s, y), :] = upc[strided(s, y), :] + fl
        loop(W, y_ends, 4)

        sent_pair(c_up, c_down)
        sent_pair(a_up, a_down)
        left(msend, mrecv, ms_s, ms_r, one)
        left(rsend, rrecv, rs_s, rs_r, one)
        left(fs, frecv, fs_s, fs_r, two)
        z_left(zmat, zm_s, zm_r)
        z_left(zrhs, zr_s, zr_r)

    flat = pltpu.VMEM((X * Y, Z), F32)
    planes = pltpu.VMEM((Y, X, Z), F32)
    flux = lambda count: pltpu.VMEM((count, Y, Z), F32)
    part = lambda *lead: pltpu.VMEM((*lead, R, Z), F32)
    sems = lambda count: pltpu.SemaphoreType.DMA((count,))
    scratch = [flat, flat, flat, flat, flat, flat, flat, flux(XB + 1), flat,
               planes, planes, planes, planes, planes, planes, planes,
               part(W, 3), part(W, 3), part(W, 2), part(W, 2), part(W), part(W), part(W + 1), part(W, 2),
               flat, flat, flat, flat, flat, flat, flat, flat,
               flux(ZB + 1), flux(ZB + 1), flux(ZB + 1), flux(ZB), flux(ZB),
               pltpu.VMEM((N, 7, Y, Z), F32), pltpu.VMEM((N, 2, Y, Z), F32), flux(N + 1), planes, planes,
               pltpu.VMEM((8, Z), F32), pltpu.VMEM((2, X, Z), F32), pltpu.VMEM((2, X, Z), F32),
               sems(W), sems(W), sems(W), sems(W), sems(W), sems(W), sems(N), sems(N), sems(N), sems(N),
               sems(2), sems(2), sems(2), sems(2), sems(4)]
    return kernel, scratch


def solution(mesh):
    W, N = mesh.shape["wide"], mesh.shape["narrow"]

    def per_device(*arrays):
        X, Y, Z = arrays[0].shape
        kernel, scratch = make_kernel(W, N, X, Y, Z)
        vmem = pl.BlockSpec(memory_space=pltpu.VMEM)
        out = jax.ShapeDtypeStruct((X * Y, Z), F32)
        results = pl.pallas_call(
            kernel,
            out_shape=(out, out),
            in_specs=[pl.BlockSpec(memory_space=pl.ANY)] * 4,
            out_specs=(vmem, vmem),
            scratch_shapes=scratch,
            compiler_params=pltpu.CompilerParams(
                collective_id=0, has_side_effects=True, vmem_limit_bytes=56 * 1024 * 1024),
        )(*[a.reshape(X * Y, Z) for a in arrays])
        return tuple(r.reshape(X, Y, Z) for r in results)

    placed = P(None, "wide", "narrow")
    return jax.shard_map(
        per_device, mesh=mesh, in_specs=(placed,) * 4, out_specs=(placed, placed), check_vma=False)
```

```python
import jax
import jax.numpy as jnp
from jax import lax
from jax.experimental import pallas as pl
from jax.experimental.pallas import tpu as pltpu
from jax.sharding import PartitionSpec as P

HALF = 256
HH = 0.5 * HALF
CELLS = 8
F32 = jnp.float32
MESH = pl.DeviceIdType.MESH


def factor(cs, lo, hi):
    n = len(cs)
    q, inv = [], []
    e = 1.0 + lo * cs[0]
    for i in range(n - 1):
        w = HH * (cs[i] + cs[i + 1])
        iv = 1.0 / (e + w)
        inv.append(iv)
        q.append(w * iv)
        e = 1.0 + q[i] * e
        if i == n - 2:
            e = e + hi * cs[n - 1]
    inv.append(1.0 / e)
    s = [None] * n
    s[1] = q[0]
    for i in range(2, n):
        s[i] = s[i - 1] * q[i - 1]
    first, last = [None] * n, [None] * n
    last[n - 1] = inv[n - 1]
    first[n - 1] = s[n - 1] * inv[n - 1]
    for i in range(n - 2, -1, -1):
        last[i] = q[i] * last[i + 1]
        first[i] = (inv[i] if i == 0 else s[i] * inv[i]) + q[i] * first[i + 1]
    return q, inv, first, last


def substitute(rs, q, inv):
    n = len(rs)
    s = [rs[0]]
    for i in range(1, n):
        s.append(rs[i] + q[i - 1] * s[i - 1])
    h = [None] * n
    h[n - 1] = s[n - 1] * inv[n - 1]
    for i in range(n - 2, -1, -1):
        h[i] = s[i] * inv[i] + q[i] * h[i + 1]
    return h


def chain_factor(diag, off):
    m, k = [], []
    for p in range(len(diag)):
        d = diag[p] if p == 0 else diag[p] - k[p - 1] * off[p - 1]
        m.append(1.0 / d)
        if p < len(off):
            k.append(m[p] * off[p])
    return m, k


def chain_solve(rhs, m, k):
    n = len(rhs)
    s = [rhs[0]]
    for p in range(1, n):
        s.append(rhs[p] + k[p - 1] * s[p - 1])
    f = [None] * n
    f[n - 1] = m[n - 1] * s[n - 1]
    for p in range(n - 2, -1, -1):
        f[p] = m[p] * s[p] + k[p] * f[p + 1]
    return f


def make_kernel(W, N, X, Y, Z):
    R = X // W
    C = W // 2
    H = X // 2
    XB, ZB = X // CELLS, Z // CELLS

    def row(ref, j):
        j = j * Y
        if not isinstance(j, int):
            j = pl.multiple_of(j, Y)
        return ref[pl.ds(j, Y), :]

    def put(ref, j, v):
        j = j * Y
        if not isinstance(j, int):
            j = pl.multiple_of(j, Y)
        ref[pl.ds(j, Y), :] = v

    def loop(count, body, unroll):
        def step(i, c):
            for u in range(unroll):
                body(i * unroll + u)
            return c
        lax.fori_loop(0, count // unroll, step, 0)

    def line_op(c_ref, v_ref, g, count, c_lo, v_lo, c_hi, v_hi):
        base = g * CELLS
        before = jnp.maximum(base - 1, 0)
        after = jnp.minimum(base + CELLS, count * CELLS - 1)
        cs = [row(c_ref, base + i) for i in range(CELLS)]
        vs = [row(v_ref, base + i) for i in range(CELLS)]
        cs = [jnp.where(g == 0, c_lo, row(c_ref, before))] + cs
        vs = [jnp.where(g == 0, v_lo, row(v_ref, before))] + vs
        cs.append(jnp.where(g == count - 1, c_hi, row(c_ref, after)))
        vs.append(jnp.where(g == count - 1, v_hi, row(v_ref, after)))
        fl = [0.5 * (cs[i] + cs[i + 1]) * (vs[i + 1] - vs[i]) for i in range(CELLS + 1)]
        return [fl[i + 1] - fl[i] for i in range(CELLS)]

    def kernel(init_h, cond_h, heat_h, known_h, adv, upc,
               init, cond, heat, known,
               hx, v1x, v8x, fx, first,
               cy, qy, iy, v1y, v8y, hy, sec,
               xs, xr, bf, ba, bb, msend, mrecv, sm, sk, fs, frecv, ps, pr,
               cz, iz, qz, nz_, v1z, v8z, hz, rz, fz, az, bz, mz, kz,
               zmat, zrhs, zf, lz, advy, ccr, chr_, ahr,
               ms_s, ms_r, fs_s, fs_r, xs_s, xs_r, ps_s, ps_r, cc_s, cc_r, zm_s, zm_r, zr_s, zr_r, ch_s, ch_r, ah_s, ah_r, in_s):
        me = lax.axis_index("wide")
        mine = lax.axis_index("narrow")
        core = lax.rem(me, 2)
        chip = me // 2
        mate = chip * 2 + 1 - core
        up = lax.rem(me + 1, W)
        down = lax.rem(me + W - 1, W)

        barrier = pltpu.get_barrier_semaphore()

        def greet(o, c):
            pl.semaphore_signal(barrier, inc=1, device_id={"wide": lax.rem(me + o, W)}, device_id_type=MESH)
            return c
        lax.fori_loop(1, W, greet, 0)
        for o in range(1, N):
            pl.semaphore_signal(barrier, inc=1, device_id={"narrow": lax.rem(mine + o, N)}, device_id_type=MESH)

        loads = [pltpu.make_async_copy(a, b, in_s.at[i]) for i, (a, b) in enumerate(
            ((cond_h, cond), (known_h, known), (init_h, init), (heat_h, heat)))]
        for load in loads:
            load.start()

        def remote(src, dst, ss, rs, **dev):
            return pltpu.make_async_remote_copy(
                src_ref=src, dst_ref=dst, send_sem=ss, recv_sem=rs, device_id=dev, device_id_type=MESH)

        lo_y = jnp.where(me == 0, HH, 0.0).astype(F32)
        hi_y = jnp.where(me == W - 1, HH, 0.0).astype(F32)

        def rows(s):
            return pl.ds(s * R, R)

        def strided(s, y):
            return pl.ds(s * (R * Y) + y, R, stride=Y)

        loads[0].wait()

        def y_matrix(s):
            cs = [cond[strided(s, y), :] for y in range(Y)]
            q, inv, a, b = factor(cs, lo_y, hi_y)
            for y in range(Y):
                cy[y, rows(s), :] = cs[y]
                if y < Y - 1:
                    qy[y, rows(s), :] = q[y]
                iy[y, rows(s), :] = inv[y]
                v1y[y, rows(s), :] = a[y]
                v8y[y, rows(s), :] = b[y]
            for i, v in enumerate((a[0], b[0], b[Y - 1], cs[0], cs[Y - 1])):
                xs[2 + i, rows(s), :] = v
        loop(W, y_matrix, 4)

        to_up = lambda src, dst, ss, rs: remote(src, dst.at[0], ss.at[0], rs.at[0], wide=up)
        to_down = lambda src, dst, ss, rs: remote(src, dst.at[1], ss.at[1], rs.at[1], wide=down)
        c_up = to_up(cy.at[Y - 1], chr_, ch_s, ch_r)
        c_down = to_down(cy.at[0], chr_, ch_s, ch_r)

        def start_pair(a, b):
            @pl.when(me < W - 1)
            def _():
                a.start()

            @pl.when(me > 0)
            def _():
                b.start()

        def recv_pair(a, b):
            @pl.when(me > 0)
            def _():
                a.wait_recv()

            @pl.when(me < W - 1)
            def _():
                b.wait_recv()

        def sent_pair(a, b):
            @pl.when(me < W - 1)
            def _():
                a.wait_send()

            @pl.when(me > 0)
            def _():
                b.wait_send()

        def zero_ends(ref):
            @pl.when(me == 0)
            def _():
                ref[0] = jnp.zeros((X, Z), F32)

            @pl.when(me == W - 1)
            def _():
                ref[1] = jnp.zeros((X, Z), F32)
        zero_ends(chr_)
        zero_ends(ahr)

        loads[1].wait()
        def x_blocks(b):
            lo = jnp.where(b == 0, HH, 0.0).astype(F32)
            hi = jnp.where(b == XB - 1, HH, 0.0).astype(F32)
            cs = [row(cond, b * CELLS + i) for i in range(CELLS)]
            rs = [(2.0 * HALF) * row(known, b * CELLS + i) for i in range(CELLS)]
            q, inv, u, v = factor(cs, lo, hi)
            h = substitute(rs, q, inv)
            for i in range(CELLS):
                put(hx, b * CELLS + i, h[i])
                put(v1x, b * CELLS + i, u[i])
                put(v8x, b * CELLS + i, v[i])
        loop(XB, x_blocks, 4)

        def exchange(send, recv, ss, rs, pick):
            def step(o, c):
                to = lax.rem(chip + o, C)
                remote(pick(send, to), recv.at[chip], ss.at[o], rs.at[o], wide=2 * to + core).start()
                return c
            lax.fori_loop(1, C, step, 0)

        def arrived(send, recv, ss, rs, pick):
            def step(o, c):
                frm = lax.rem(chip + C - o, C)
                remote(pick(send, frm), recv.at[frm], ss.at[o], rs.at[o], wide=2 * frm + core).wait_recv()
                return c
            lax.fori_loop(1, C, step, 0)

        def left(send, recv, ss, rs, pick):
            def step(o, c):
                to = lax.rem(chip + o, C)
                remote(pick(send, to), recv.at[chip], ss.at[o], rs.at[o], wide=2 * to + core).wait_send()
                return c
            lax.fori_loop(1, C, step, 0)

        one = lambda ref, s: ref.at[s]
        two = lambda ref, s: ref.at[pl.ds(s, 2)]
        def inner(c_ref, a_ref, b_ref, blocks):
            diag, off = [], []
            for p in range(1, blocks):
                j = p * CELLS
                w = HH * (row(c_ref, j - 1) + row(c_ref, j))
                diag.append(1.0 / w + row(b_ref, j - 1) + row(a_ref, j))
                if p < blocks - 1:
                    off.append(row(b_ref, j))
            return chain_factor(diag, off)

        zero = jnp.zeros((Y, Z), F32)
        m, k = inner(cond, v1x, v8x, XB)
        f = chain_solve([row(hx, p * CELLS - 1) - row(hx, p * CELLS) for p in range(1, XB)], m, k)
        fx[0] = zero
        fx[XB] = zero
        for p in range(1, XB):
            fx[p] = f[p - 1]

        def x_final(b):
            fl, fr = fx[b], fx[b + 1]
            for i in range(CELLS):
                j = b * CELLS + i
                put(first, j, row(hx, j) + row(v1x, j) * fl - row(v8x, j) * fr)
        loop(XB, x_final, 4)

        def y_rhs(s):
            rs = [first[strided(s, y), :] for y in range(Y)]
            h = substitute(rs, [qy[y, rows(s), :] for y in range(Y - 1)], [iy[y, rows(s), :] for y in range(Y)])
            for y in range(Y):
                hy[y, rows(s), :] = h[y]
            xs[0, rows(s), :] = h[0]
            xs[1, rows(s), :] = h[Y - 1]
        loop(W, y_rhs, 4)
        pl.semaphore_wait(barrier, W - 1 + N - 1)
        side, far = pl.multiple_of(core * H, H), pl.multiple_of((1 - core) * H, H)
        to_mate = remote(xs.at[:, pl.ds(far, H), :], xr, xs_s.at[0], xs_r.at[0], wide=mate)
        to_mate.start()
        skip = remote(cy.at[Y - 1, pl.ds(H, H), :], ccr, cc_s.at[0], cc_r.at[0], wide=lax.rem(me + 2, W))
        skip_sends = jnp.logical_and(core == 1, me < W - 2)
        skip_comes = jnp.logical_and(core == 1, me > 2)

        @pl.when(skip_sends)
        def _():
            skip.start()
        start_pair(c_up, c_down)

        recv_pair(c_up, c_down)

        @pl.when(core == 0)
        def _():
            ccr[...] = chr_[0, pl.ds(0, H), :]

        @pl.when(skip_comes)
        def _():
            skip.wait_recv()

        @pl.when(me == 1)
        def _():
            ccr[...] = jnp.zeros((H, Z), F32)
        to_mate.wait_recv()
        is_low = core == 0

        def merge(g):
            at = pl.ds(g * R, R)
            own = [xs[i, pl.ds(side + g * R, R), :] for i in range(7)]
            oth = [xr[i, at, :] for i in range(7)]
            h1, h8, g1, gx, g8, c1, c8 = [jnp.where(is_low, a, b) for a, b in zip(own, oth)]
            k1, k8, j1, jx, j8, d1, d8 = [jnp.where(is_low, b, a) for a, b in zip(own, oth)]
            m = 1.0 / (1.0 / (HH * (c8 + d1)) + g8 + j1)
            f = m * (h8 - k1)
            alpha, beta = m * gx, m * jx
            bf[at, :] = f
            ba[at, :] = alpha
            bb[at, :] = beta
            msend[g, 0] = h1 - gx * f
            msend[g, 1] = k8 + jx * f
            msend[g, 2] = g1 - gx * alpha + 1.0 / (HH * (ccr[at, :] + c1))
            msend[g, 3] = j8 - jx * beta
            msend[g, 4] = jx * alpha
        loop(C, merge, 4)
        exchange(msend, mrecv, ms_s, ms_r, one)
        mrecv[chip] = msend[chip]

        loads[2].wait()
        for y in range(Y):
            cz[pl.ds(y, Z, stride=Y), :] = cy[y].T
            iz[pl.ds(y, Z, stride=Y), :] = init[pl.ds(y, X, stride=Y), :].T
        lo_z = jnp.where(mine == 0, HH, 0.0).astype(F32)
        hi_z = jnp.where(mine == N - 1, HH, 0.0).astype(F32)

        def z_blocks(b):
            lo = jnp.where(b == 0, lo_z, 0.0)
            hi = jnp.where(b == ZB - 1, hi_z, 0.0)
            cs = [row(cz, b * CELLS + i) for i in range(CELLS)]
            q, inv, u, v = factor(cs, lo, hi)
            for i in range(CELLS):
                j = b * CELLS + i
                if i < CELLS - 1:
                    put(qz, j, q[i])
                put(nz_, j, inv[i])
                put(v1z, j, u[i])
                put(v8z, j, v[i])
        loop(ZB, z_blocks, 4)
        m, k = inner(cz, v1z, v8z, ZB)
        n = ZB - 1
        for p in range(n):
            mz[p] = m[p]
            if p < n - 1:
                kz[p] = k[p]
        g18_lo, g18_hi = row(v8z, 0), row(v8z, (ZB - 1) * CELLS)
        a = chain_solve([g18_lo] + [zero] * (n - 1), m, k)
        b = [None] * n
        b[n - 1] = m[n - 1] * g18_hi
        for p in range(n - 2, -1, -1):
            b[p] = k[p] * b[p + 1]
        for p in range(n):
            az[p + 1] = a[p]
            bz[p + 1] = b[p]
        one_plane = jnp.ones((Y, Z), F32)
        az[0], bz[0] = one_plane, zero
        az[ZB], bz[ZB] = zero, one_plane
        zmat[mine, 0] = row(v1z, 0) - g18_lo * a[0]
        zmat[mine, 1] = row(v8z, Z - 1) - g18_hi * b[n - 1]
        zmat[mine, 2] = g18_hi * a[n - 1]
        zmat[mine, 3] = row(cz, 0)
        zmat[mine, 4] = row(cz, Z - 1)
        zmat[mine, 5] = row(iz, 0)
        zmat[mine, 6] = row(iz, Z - 1)

        def z_copy(buf, ss, rs, o, who, slot):
            return remote(buf.at[slot], buf.at[slot], ss.at[o], rs.at[o], narrow=who)

        def z_send(buf, ss, rs):
            for o in range(1, N):
                z_copy(buf, ss, rs, o, lax.rem(mine + o, N), mine).start()

        def z_recv(buf, ss, rs):
            for o in range(1, N):
                frm = lax.rem(mine + N - o, N)
                z_copy(buf, ss, rs, o, frm, frm).wait_recv()

        def z_left(buf, ss, rs):
            for o in range(1, N):
                z_copy(buf, ss, rs, o, lax.rem(mine + o, N), mine).wait_send()
        z_send(zmat, zm_s, zm_r)

        z_recv(zmat, zm_s, zm_r)
        below, above = jnp.maximum(mine - 1, 0), jnp.minimum(mine + 1, N - 1)
        has_lo = jnp.where(mine > 0, 1.0, 0.0).astype(F32)
        has_hi = jnp.where(mine < N - 1, 1.0, 0.0).astype(F32)
        z_c_lo, z_v_lo = has_lo * zmat[below, 4], has_lo * zmat[below, 6]
        z_c_hi, z_v_hi = has_hi * zmat[above, 3], has_hi * zmat[above, 5]

        def z_old(g):
            out = line_op(cz, iz, g, ZB, z_c_lo, z_v_lo, z_c_hi, z_v_hi)
            for i in range(CELLS):
                put(rz, g * CELLS + i, out[i])
        loop(ZB, z_old, 2)
        for y in range(Y):
            lz[y] = rz[pl.ds(y, Z, stride=Y), :].T

        arrived(msend, mrecv, ms_s, ms_r, one)
        m, k = chain_factor(
            [mrecv[p, 2] + mrecv[p - 1, 3] for p in range(1, C)], [mrecv[p, 4] for p in range(1, C - 1)])
        f = chain_solve([mrecv[p - 1, 1] - mrecv[p, 0] for p in range(1, C)], m, k)
        edge = jnp.zeros((R, Z), F32)
        fs[0] = edge
        fs[C] = edge
        for p in range(1, C):
            fs[p] = f[p - 1]
        exchange(fs, frecv, fs_s, fs_r, two)
        frecv[chip] = fs[pl.ds(chip, 2)]
        arrived(fs, frecv, fs_s, fs_r, two)

        def finish(at, fl, fr):
            for y in range(Y):
                sec[y, at, :] = hy[y, at, :] + v1y[y, at, :] * fl - v8y[y, at, :] * fr

        def middle(g):
            at = pl.ds(g * R, R)
            fl, fr = frecv[g, 0], frecv[g, 1]
            f = bf[at, :] + ba[at, :] * fl + bb[at, :] * fr
            ps[0, at, :] = jnp.where(is_low, f, fl)
            ps[1, at, :] = jnp.where(is_low, fr, f)
        loop(C, middle, 4)
        flux_mate = remote(ps, pr, ps_s.at[0], ps_r.at[0], wide=mate)
        flux_mate.start()

        def own_final(g):
            fl, fr = frecv[g, 0], frecv[g, 1]
            at = pl.ds(g * R, R)
            f = jnp.where(is_low, ps[0, at, :], ps[1, at, :])
            finish(pl.ds(side + g * R, R), jnp.where(is_low, fl, f), jnp.where(is_low, f, fr))
        loop(C, own_final, 4)
        flux_mate.wait_recv()

        def mate_final(g):
            at = pl.ds(g * R, R)
            finish(pl.ds(far + g * R, R), pr[0, at, :], pr[1, at, :])
        loop(C, mate_final, 4)
        for y in range(Y):
            rz[pl.ds(y, Z, stride=Y), :] = sec[y].T

        def z_rhs(b):
            j = b * CELLS
            h = substitute([row(rz, j + i) for i in range(CELLS)], [row(qz, j + i) for i in range(CELLS - 1)],
                           [row(nz_, j + i) for i in range(CELLS)])
            for i in range(CELLS):
                put(hz, j + i, h[i])
        loop(ZB, z_rhs, 4)
        f = chain_solve([row(hz, p * CELLS - 1) - row(hz, p * CELLS) for p in range(1, ZB)],
                        [mz[p] for p in range(n)], [kz[p] for p in range(n - 1)])
        for p in range(n):
            fz[p + 1] = f[p]
        fz[0] = zero
        fz[ZB] = zero
        zrhs[mine, 0] = row(hz, 0) - row(v8z, 0) * f[0]
        zrhs[mine, 1] = row(hz, Z - 1) + row(v8z, (ZB - 1) * CELLS) * f[n - 1]
        z_send(zrhs, zr_s, zr_r)
        m, k = chain_factor(
            [1.0 / (HH * (zmat[p - 1, 4] + zmat[p, 3])) + zmat[p - 1, 1] + zmat[p, 0] for p in range(1, N)],
            [zmat[p, 2] for p in range(1, N - 1)])
        z_recv(zrhs, zr_s, zr_r)
        f = chain_solve([zrhs[p - 1, 1] - zrhs[p, 0] for p in range(1, N)], m, k)
        zf[0] = zero
        zf[N] = zero
        for p in range(1, N):
            zf[p] = f[p - 1]
        z_fl, z_fr = zf[mine], zf[mine + 1]

        def z_final(b):
            fl = fz[b] + az[b] * z_fl + bz[b] * z_fr
            fr = fz[b + 1] + az[b + 1] * z_fl + bz[b + 1] * z_fr
            for i in range(CELLS):
                j = b * CELLS + i
                put(rz, j, row(hz, j) + row(v1z, j) * fl - row(v8z, j) * fr)
        loop(ZB, z_final, 4)

        a_up = to_up(advy.at[Y - 1], ahr, ah_s, ah_r)
        a_down = to_down(advy.at[0], ahr, ah_s, ah_r)

        def new_state(y):
            third = rz[pl.ds(y, Z, stride=Y), :].T
            state = init[pl.ds(y, X, stride=Y), :] + third
            advy[y] = state
            lz[y] = lz[y] + (third - sec[y]) * (1.0 / HALF)
            adv[pl.ds(y, X, stride=Y), :] = state
        new_state(0)
        new_state(Y - 1)
        start_pair(a_up, a_down)
        for y in range(1, Y - 1):
            new_state(y)

        def y_op(s):
            cs = [cy[y, rows(s), :] for y in range(Y)]
            vs = [advy[y, rows(s), :] for y in range(Y)]
            fl = [0.5 * (cs[i] + cs[i + 1]) * (vs[i + 1] - vs[i]) for i in range(Y - 1)]
            for y in range(Y):
                out = lz[y, rows(s), :]
                if y < Y - 1:
                    out = out + fl[y]
                if y > 0:
                    out = out - fl[y - 1]
                upc[strided(s, y), :] = out
        loop(W, y_op, 4)

        loads[3].wait()

        def x_op(g):
            out = line_op(cond, adv, g, XB, zero, zero, zero, zero)
            for i in range(CELLS):
                j = g * CELLS + i
                put(upc, j, row(upc, j) + (row(heat, j) + out[i]))
        loop(XB, x_op, 2)

        recv_pair(a_up, a_down)

        def y_ends(s):
            for slot, y in ((0, 0), (1, Y - 1)):
                fl = 0.5 * (chr_[slot, rows(s), :] + cy[y, rows(s), :]) * (ahr[slot, rows(s), :] - advy[y, rows(s), :])
                upc[strided(s, y), :] = upc[strided(s, y), :] + fl
        loop(W, y_ends, 4)

        sent_pair(c_up, c_down)
        sent_pair(a_up, a_down)
        left(msend, mrecv, ms_s, ms_r, one)
        to_mate.wait_send()
        flux_mate.wait_send()

        @pl.when(skip_sends)
        def _():
            skip.wait_send()
        left(fs, frecv, fs_s, fs_r, two)
        z_left(zmat, zm_s, zm_r)
        z_left(zrhs, zr_s, zr_r)

    flat = pltpu.VMEM((X * Y, Z), F32)
    planes = pltpu.VMEM((Y, X, Z), F32)
    flux = lambda count: pltpu.VMEM((count, Y, Z), F32)
    part = lambda *lead: pltpu.VMEM((*lead, R, Z), F32)
    half = lambda *lead: pltpu.VMEM((*lead, H, Z), F32)
    sems = lambda count: pltpu.SemaphoreType.DMA((count,))
    scratch = [flat, flat, flat, flat, flat, flat, flat, flux(XB + 1), flat,
               planes, planes, planes, planes, planes, planes, planes,
               pltpu.VMEM((7, X, Z), F32), pltpu.VMEM((7, H, Z), F32), half(), half(), half(),
               part(C, 5), part(C, 5), part(C), part(C), part(C + 1), part(C, 2), half(2), half(2),
               flat, flat, flat, flat, flat, flat, flat, flat,
               flux(ZB + 1), flux(ZB + 1), flux(ZB + 1), flux(ZB), flux(ZB),
               pltpu.VMEM((N, 7, Y, Z), F32), pltpu.VMEM((N, 2, Y, Z), F32), flux(N + 1), planes, planes,
               half(), pltpu.VMEM((2, X, Z), F32), pltpu.VMEM((2, X, Z), F32),
               sems(C), sems(C), sems(C), sems(C), sems(1), sems(1), sems(1), sems(1), sems(1), sems(1), sems(N), sems(N), sems(N), sems(N),
               sems(2), sems(2), sems(2), sems(2), sems(4)]
    return kernel, scratch


def solution(mesh):
    W, N = mesh.shape["wide"], mesh.shape["narrow"]

    def per_device(*arrays):
        X, Y, Z = arrays[0].shape
        kernel, scratch = make_kernel(W, N, X, Y, Z)
        vmem = pl.BlockSpec(memory_space=pltpu.VMEM)
        out = jax.ShapeDtypeStruct((X * Y, Z), F32)
        results = pl.pallas_call(
            kernel,
            out_shape=(out, out),
            in_specs=[pl.BlockSpec(memory_space=pltpu.HBM)] * 4,
            out_specs=(vmem, vmem),
            scratch_shapes=scratch,
            compiler_params=pltpu.CompilerParams(
                collective_id=0, has_side_effects=True, vmem_limit_bytes=56 * 1024 * 1024),
        )(*[a.reshape(X * Y, Z) for a in arrays])
        return tuple(r.reshape(X, Y, Z) for r in results)

    placed = P(None, "wide", "narrow")
    return jax.shard_map(
        per_device, mesh=mesh, in_specs=(placed,) * 4, out_specs=(placed, placed), check_vma=False)
```

```python
import jax
import jax.numpy as jnp
from jax import lax
from jax.experimental import pallas as pl
from jax.experimental.pallas import tpu as pltpu
from jax.sharding import PartitionSpec as P

HALF = 256
HH = 0.5 * HALF
CELLS = 8
F32 = jnp.float32
MESH = pl.DeviceIdType.MESH


def factor(cs, lo, hi):
    n = len(cs)
    q, inv = [], []
    e = 1.0 + lo * cs[0]
    for i in range(n - 1):
        w = HH * (cs[i] + cs[i + 1])
        iv = 1.0 / (e + w)
        inv.append(iv)
        q.append(w * iv)
        e = 1.0 + q[i] * e
        if i == n - 2:
            e = e + hi * cs[n - 1]
    inv.append(1.0 / e)
    s = [None] * n
    s[1] = q[0]
    for i in range(2, n):
        s[i] = s[i - 1] * q[i - 1]
    first, last = [None] * n, [None] * n
    last[n - 1] = inv[n - 1]
    first[n - 1] = s[n - 1] * inv[n - 1]
    for i in range(n - 2, -1, -1):
        last[i] = q[i] * last[i + 1]
        first[i] = (inv[i] if i == 0 else s[i] * inv[i]) + q[i] * first[i + 1]
    return q, inv, first, last


def substitute(rs, q, inv):
    n = len(rs)
    s = [rs[0]]
    for i in range(1, n):
        s.append(rs[i] + q[i - 1] * s[i - 1])
    h = [None] * n
    h[n - 1] = s[n - 1] * inv[n - 1]
    for i in range(n - 2, -1, -1):
        h[i] = s[i] * inv[i] + q[i] * h[i + 1]
    return h


def chain_factor(diag, off):
    m, k = [], []
    for p in range(len(diag)):
        d = diag[p] if p == 0 else diag[p] - k[p - 1] * off[p - 1]
        m.append(1.0 / d)
        if p < len(off):
            k.append(m[p] * off[p])
    return m, k


def chain_solve(rhs, m, k):
    n = len(rhs)
    s = [rhs[0]]
    for p in range(1, n):
        s.append(rhs[p] + k[p - 1] * s[p - 1])
    f = [None] * n
    f[n - 1] = m[n - 1] * s[n - 1]
    for p in range(n - 2, -1, -1):
        f[p] = m[p] * s[p] + k[p] * f[p + 1]
    return f


def make_kernel(W, N, X, Y, Z):
    R = X // W
    C = W // 2
    H = X // 2
    XB, ZB = X // CELLS, Z // CELLS

    def row(ref, j):
        j = j * Y
        if not isinstance(j, int):
            j = pl.multiple_of(j, Y)
        return ref[pl.ds(j, Y), :]

    def put(ref, j, v):
        j = j * Y
        if not isinstance(j, int):
            j = pl.multiple_of(j, Y)
        ref[pl.ds(j, Y), :] = v

    def loop(count, body, unroll):
        def step(i, c):
            for u in range(unroll):
                body(i * unroll + u)
            return c
        lax.fori_loop(0, count // unroll, step, 0)

    def line_op(c_ref, v_ref, g, count, c_lo, v_lo, c_hi, v_hi):
        base = g * CELLS
        before = jnp.maximum(base - 1, 0)
        after = jnp.minimum(base + CELLS, count * CELLS - 1)
        cs = [row(c_ref, base + i) for i in range(CELLS)]
        vs = [row(v_ref, base + i) for i in range(CELLS)]
        cs = [jnp.where(g == 0, c_lo, row(c_ref, before))] + cs
        vs = [jnp.where(g == 0, v_lo, row(v_ref, before))] + vs
        cs.append(jnp.where(g == count - 1, c_hi, row(c_ref, after)))
        vs.append(jnp.where(g == count - 1, v_hi, row(v_ref, after)))
        fl = [0.5 * (cs[i] + cs[i + 1]) * (vs[i + 1] - vs[i]) for i in range(CELLS + 1)]
        return [fl[i + 1] - fl[i] for i in range(CELLS)]

    def kernel(init_h, cond_h, heat_h, known_h, adv, upc,
               init, cond, heat, known,
               hx, v1x, v8x, fx, first,
               cy, qy, iy, v1y, v8y, hy, sec,
               xs, xr, bf, ba, bb, msend, mrecv, sm, sk, fs, frecv, ps, pr,
               cz, iz, qz, nz_, v1z, v8z, hz, rz, fz, az, bz, mz, kz,
               zmat, zrhs, zf, lz, advy, ccr, chr_, ahr,
               ms_s, ms_r, fs_s, fs_r, xs_s, xs_r, ps_s, ps_r, cc_s, cc_r, zm_s, zm_r, zr_s, zr_r, ch_s, ch_r, ah_s, ah_r, in_s):
        me = lax.axis_index("wide")
        mine = lax.axis_index("narrow")
        core = lax.rem(me, 2)
        chip = me // 2
        mate = chip * 2 + 1 - core
        up = lax.rem(me + 1, W)
        down = lax.rem(me + W - 1, W)

        barrier = pltpu.get_barrier_semaphore()

        def greet(o, c):
            pl.semaphore_signal(barrier, inc=1, device_id={"wide": lax.rem(me + o, W)}, device_id_type=MESH)
            return c
        lax.fori_loop(1, W, greet, 0)
        for o in range(1, N):
            pl.semaphore_signal(barrier, inc=1, device_id={"narrow": lax.rem(mine + o, N)}, device_id_type=MESH)

        loads = [pltpu.make_async_copy(a, b, in_s.at[i]) for i, (a, b) in enumerate(
            ((cond_h, cond), (known_h, known), (init_h, init), (heat_h, heat)))]
        for load in loads:
            load.start()

        def remote(src, dst, ss, rs, **dev):
            return pltpu.make_async_remote_copy(
                src_ref=src, dst_ref=dst, send_sem=ss, recv_sem=rs, device_id=dev, device_id_type=MESH)

        lo_y = jnp.where(me == 0, HH, 0.0).astype(F32)
        hi_y = jnp.where(me == W - 1, HH, 0.0).astype(F32)

        def rows(s):
            return pl.ds(s * R, R)

        def strided(s, y):
            return pl.ds(s * (R * Y) + y, R, stride=Y)

        loads[0].wait()

        def y_matrix(s):
            cs = [cond[strided(s, y), :] for y in range(Y)]
            q, inv, a, b = factor(cs, lo_y, hi_y)
            for y in range(Y):
                cy[y, rows(s), :] = cs[y]
                if y < Y - 1:
                    qy[y, rows(s), :] = q[y]
                iy[y, rows(s), :] = inv[y]
                v1y[y, rows(s), :] = a[y]
                v8y[y, rows(s), :] = b[y]
            for i, v in enumerate((a[0], b[0], b[Y - 1], cs[0], cs[Y - 1])):
                xs[2 + i, rows(s), :] = v
        loop(W, y_matrix, 4)

        to_up = lambda src, dst, ss, rs: remote(src, dst.at[0], ss.at[0], rs.at[0], wide=up)
        to_down = lambda src, dst, ss, rs: remote(src, dst.at[1], ss.at[1], rs.at[1], wide=down)
        c_up = to_up(cy.at[Y - 1], chr_, ch_s, ch_r)
        c_down = to_down(cy.at[0], chr_, ch_s, ch_r)

        def start_pair(a, b):
            @pl.when(me < W - 1)
            def _():
                a.start()

            @pl.when(me > 0)
            def _():
                b.start()

        def recv_pair(a, b):
            @pl.when(me > 0)
            def _():
                a.wait_recv()

            @pl.when(me < W - 1)
            def _():
                b.wait_recv()

        def sent_pair(a, b):
            @pl.when(me < W - 1)
            def _():
                a.wait_send()

            @pl.when(me > 0)
            def _():
                b.wait_send()

        def zero_ends(ref):
            @pl.when(me == 0)
            def _():
                ref[0] = jnp.zeros((X, Z), F32)

            @pl.when(me == W - 1)
            def _():
                ref[1] = jnp.zeros((X, Z), F32)
        zero_ends(chr_)
        zero_ends(ahr)

        loads[1].wait()
        def x_blocks(b):
            lo = jnp.where(b == 0, HH, 0.0).astype(F32)
            hi = jnp.where(b == XB - 1, HH, 0.0).astype(F32)
            cs = [row(cond, b * CELLS + i) for i in range(CELLS)]
            rs = [(2.0 * HALF) * row(known, b * CELLS + i) for i in range(CELLS)]
            q, inv, u, v = factor(cs, lo, hi)
            h = substitute(rs, q, inv)
            for i in range(CELLS):
                put(hx, b * CELLS + i, h[i])
                put(v1x, b * CELLS + i, u[i])
                put(v8x, b * CELLS + i, v[i])
        loop(XB, x_blocks, 4)

        def exchange(send, recv, ss, rs, pick):
            def step(o, c):
                to = lax.rem(chip + o, C)
                remote(pick(send, to), recv.at[chip], ss.at[o], rs.at[o], wide=2 * to + core).start()
                return c
            lax.fori_loop(1, C, step, 0)

        def arrived(send, recv, ss, rs, pick):
            def step(o, c):
                frm = lax.rem(chip + C - o, C)
                remote(pick(send, frm), recv.at[frm], ss.at[o], rs.at[o], wide=2 * frm + core).wait_recv()
                return c
            lax.fori_loop(1, C, step, 0)

        def left(send, recv, ss, rs, pick):
            def step(o, c):
                to = lax.rem(chip + o, C)
                remote(pick(send, to), recv.at[chip], ss.at[o], rs.at[o], wide=2 * to + core).wait_send()
                return c
            lax.fori_loop(1, C, step, 0)

        one = lambda ref, s: ref.at[s]
        two = lambda ref, s: ref.at[pl.ds(s, 2)]
        def inner(c_ref, a_ref, b_ref, blocks):
            diag, off = [], []
            for p in range(1, blocks):
                j = p * CELLS
                w = HH * (row(c_ref, j - 1) + row(c_ref, j))
                diag.append(1.0 / w + row(b_ref, j - 1) + row(a_ref, j))
                if p < blocks - 1:
                    off.append(row(b_ref, j))
            return chain_factor(diag, off)

        zero = jnp.zeros((Y, Z), F32)
        m, k = inner(cond, v1x, v8x, XB)
        f = chain_solve([row(hx, p * CELLS - 1) - row(hx, p * CELLS) for p in range(1, XB)], m, k)
        fx[0] = zero
        fx[XB] = zero
        for p in range(1, XB):
            fx[p] = f[p - 1]

        def x_final(b):
            fl, fr = fx[b], fx[b + 1]
            for i in range(CELLS):
                j = b * CELLS + i
                put(first, j, row(hx, j) + row(v1x, j) * fl - row(v8x, j) * fr)
        loop(XB, x_final, 4)

        def y_rhs(s):
            rs = [first[strided(s, y), :] for y in range(Y)]
            h = substitute(rs, [qy[y, rows(s), :] for y in range(Y - 1)], [iy[y, rows(s), :] for y in range(Y)])
            for y in range(Y):
                hy[y, rows(s), :] = h[y]
            xs[0, rows(s), :] = h[0]
            xs[1, rows(s), :] = h[Y - 1]
        loop(W, y_rhs, 4)
        pl.semaphore_wait(barrier, W - 1 + N - 1)
        side, far = pl.multiple_of(core * H, H), pl.multiple_of((1 - core) * H, H)
        to_mate = remote(xs.at[:, pl.ds(far, H), :], xr, xs_s.at[0], xs_r.at[0], wide=mate)
        to_mate.start()
        skip = remote(cy.at[Y - 1, pl.ds(H, H), :], ccr, cc_s.at[0], cc_r.at[0], wide=lax.rem(me + 2, W))
        skip_sends = jnp.logical_and(core == 1, me < W - 2)
        skip_comes = jnp.logical_and(core == 1, me > 2)

        @pl.when(skip_sends)
        def _():
            skip.start()
        start_pair(c_up, c_down)

        recv_pair(c_up, c_down)

        @pl.when(core == 0)
        def _():
            ccr[...] = chr_[0, pl.ds(0, H), :]

        @pl.when(skip_comes)
        def _():
            skip.wait_recv()

        @pl.when(me == 1)
        def _():
            ccr[...] = jnp.zeros((H, Z), F32)
        to_mate.wait_recv()
        is_low = core == 0

        def merge(g):
            at = pl.ds(g * R, R)
            own = [xs[i, pl.ds(side + g * R, R), :] for i in range(7)]
            oth = [xr[i, at, :] for i in range(7)]
            h1, h8, g1, gx, g8, c1, c8 = [jnp.where(is_low, a, b) for a, b in zip(own, oth)]
            k1, k8, j1, jx, j8, d1, d8 = [jnp.where(is_low, b, a) for a, b in zip(own, oth)]
            m = 1.0 / (1.0 / (HH * (c8 + d1)) + g8 + j1)
            f = m * (h8 - k1)
            alpha, beta = m * gx, m * jx
            bf[at, :] = f
            ba[at, :] = alpha
            bb[at, :] = beta
            msend[g, 0] = h1 - gx * f
            msend[g, 1] = k8 + jx * f
            msend[g, 2] = g1 - gx * alpha + 1.0 / (HH * (ccr[at, :] + c1))
            msend[g, 3] = j8 - jx * beta
            msend[g, 4] = jx * alpha
        loop(C, merge, 4)
        exchange(msend, mrecv, ms_s, ms_r, one)
        mrecv[chip] = msend[chip]

        loads[2].wait()
        for y in range(Y):
            cz[pl.ds(y, Z, stride=Y), :] = cy[y].T
            iz[pl.ds(y, Z, stride=Y), :] = init[pl.ds(y, X, stride=Y), :].T
        lo_z = jnp.where(mine == 0, HH, 0.0).astype(F32)
        hi_z = jnp.where(mine == N - 1, HH, 0.0).astype(F32)

        def z_blocks(b):
            lo = jnp.where(b == 0, lo_z, 0.0)
            hi = jnp.where(b == ZB - 1, hi_z, 0.0)
            cs = [row(cz, b * CELLS + i) for i in range(CELLS)]
            q, inv, u, v = factor(cs, lo, hi)
            for i in range(CELLS):
                j = b * CELLS + i
                if i < CELLS - 1:
                    put(qz, j, q[i])
                put(nz_, j, inv[i])
                put(v1z, j, u[i])
                put(v8z, j, v[i])
        loop(ZB, z_blocks, 4)
        m, k = inner(cz, v1z, v8z, ZB)
        n = ZB - 1
        for p in range(n):
            mz[p] = m[p]
            if p < n - 1:
                kz[p] = k[p]
        g18_lo, g18_hi = row(v8z, 0), row(v8z, (ZB - 1) * CELLS)
        a = chain_solve([g18_lo] + [zero] * (n - 1), m, k)
        b = [None] * n
        b[n - 1] = m[n - 1] * g18_hi
        for p in range(n - 2, -1, -1):
            b[p] = k[p] * b[p + 1]
        for p in range(n):
            az[p + 1] = a[p]
            bz[p + 1] = b[p]
        one_plane = jnp.ones((Y, Z), F32)
        az[0], bz[0] = one_plane, zero
        az[ZB], bz[ZB] = zero, one_plane
        zmat[mine, 0] = row(v1z, 0) - g18_lo * a[0]
        zmat[mine, 1] = row(v8z, Z - 1) - g18_hi * b[n - 1]
        zmat[mine, 2] = g18_hi * a[n - 1]
        zmat[mine, 3] = row(cz, 0)
        zmat[mine, 4] = row(cz, Z - 1)
        zmat[mine, 5] = row(iz, 0)
        zmat[mine, 6] = row(iz, Z - 1)

        def z_copy(buf, ss, rs, o, who, slot):
            return remote(buf.at[slot], buf.at[slot], ss.at[o], rs.at[o], narrow=who)

        def z_send(buf, ss, rs):
            for o in range(1, N):
                z_copy(buf, ss, rs, o, lax.rem(mine + o, N), mine).start()

        def z_recv(buf, ss, rs):
            for o in range(1, N):
                frm = lax.rem(mine + N - o, N)
                z_copy(buf, ss, rs, o, frm, frm).wait_recv()

        def z_left(buf, ss, rs):
            for o in range(1, N):
                z_copy(buf, ss, rs, o, lax.rem(mine + o, N), mine).wait_send()
        z_send(zmat, zm_s, zm_r)

        z_recv(zmat, zm_s, zm_r)
        below, above = jnp.maximum(mine - 1, 0), jnp.minimum(mine + 1, N - 1)
        has_lo = jnp.where(mine > 0, 1.0, 0.0).astype(F32)
        has_hi = jnp.where(mine < N - 1, 1.0, 0.0).astype(F32)
        z_c_lo, z_v_lo = has_lo * zmat[below, 4], has_lo * zmat[below, 6]
        z_c_hi, z_v_hi = has_hi * zmat[above, 3], has_hi * zmat[above, 5]

        def z_old(g):
            out = line_op(cz, iz, g, ZB, z_c_lo, z_v_lo, z_c_hi, z_v_hi)
            for i in range(CELLS):
                put(rz, g * CELLS + i, out[i])
        loop(ZB, z_old, 2)
        for y in range(Y):
            lz[y] = rz[pl.ds(y, Z, stride=Y), :].T

        arrived(msend, mrecv, ms_s, ms_r, one)
        m, k = chain_factor(
            [mrecv[p, 2] + mrecv[p - 1, 3] for p in range(1, C)], [mrecv[p, 4] for p in range(1, C - 1)])
        f = chain_solve([mrecv[p - 1, 1] - mrecv[p, 0] for p in range(1, C)], m, k)
        edge = jnp.zeros((R, Z), F32)
        fs[0] = edge
        fs[C] = edge
        for p in range(1, C):
            fs[p] = f[p - 1]
        exchange(fs, frecv, fs_s, fs_r, two)
        frecv[chip] = fs[pl.ds(chip, 2)]
        arrived(fs, frecv, fs_s, fs_r, two)

        def finish(at, fl, fr):
            for y in range(Y):
                sec[y, at, :] = hy[y, at, :] + v1y[y, at, :] * fl - v8y[y, at, :] * fr

        def middle(g):
            at = pl.ds(g * R, R)
            fl, fr = frecv[g, 0], frecv[g, 1]
            f = bf[at, :] + ba[at, :] * fl + bb[at, :] * fr
            ps[0, at, :] = jnp.where(is_low, f, fl)
            ps[1, at, :] = jnp.where(is_low, fr, f)
        loop(C, middle, 4)
        flux_mate = remote(ps, pr, ps_s.at[0], ps_r.at[0], wide=mate)
        flux_mate.start()

        def own_final(g):
            fl, fr = frecv[g, 0], frecv[g, 1]
            at = pl.ds(g * R, R)
            f = jnp.where(is_low, ps[0, at, :], ps[1, at, :])
            finish(pl.ds(side + g * R, R), jnp.where(is_low, fl, f), jnp.where(is_low, f, fr))
        loop(C, own_final, 4)
        flux_mate.wait_recv()

        def mate_final(g):
            at = pl.ds(g * R, R)
            finish(pl.ds(far + g * R, R), pr[0, at, :], pr[1, at, :])
        loop(C, mate_final, 4)
        for y in range(Y):
            rz[pl.ds(y, Z, stride=Y), :] = sec[y].T

        def z_rhs(b):
            j = b * CELLS
            h = substitute([row(rz, j + i) for i in range(CELLS)], [row(qz, j + i) for i in range(CELLS - 1)],
                           [row(nz_, j + i) for i in range(CELLS)])
            for i in range(CELLS):
                put(hz, j + i, h[i])
        loop(ZB, z_rhs, 4)
        f = chain_solve([row(hz, p * CELLS - 1) - row(hz, p * CELLS) for p in range(1, ZB)],
                        [mz[p] for p in range(n)], [kz[p] for p in range(n - 1)])
        for p in range(n):
            fz[p + 1] = f[p]
        fz[0] = zero
        fz[ZB] = zero
        zrhs[mine, 0] = row(hz, 0) - row(v8z, 0) * f[0]
        zrhs[mine, 1] = row(hz, Z - 1) + row(v8z, (ZB - 1) * CELLS) * f[n - 1]
        z_send(zrhs, zr_s, zr_r)
        m, k = chain_factor(
            [1.0 / (HH * (zmat[p - 1, 4] + zmat[p, 3])) + zmat[p - 1, 1] + zmat[p, 0] for p in range(1, N)],
            [zmat[p, 2] for p in range(1, N - 1)])
        z_recv(zrhs, zr_s, zr_r)
        f = chain_solve([zrhs[p - 1, 1] - zrhs[p, 0] for p in range(1, N)], m, k)
        zf[0] = zero
        zf[N] = zero
        for p in range(1, N):
            zf[p] = f[p - 1]
        z_fl, z_fr = zf[mine], zf[mine + 1]

        def z_final(b):
            fl = fz[b] + az[b] * z_fl + bz[b] * z_fr
            fr = fz[b + 1] + az[b + 1] * z_fl + bz[b + 1] * z_fr
            for i in range(CELLS):
                j = b * CELLS + i
                put(rz, j, row(hz, j) + row(v1z, j) * fl - row(v8z, j) * fr)
        loop(ZB, z_final, 4)

        a_up = to_up(advy.at[Y - 1], ahr, ah_s, ah_r)
        a_down = to_down(advy.at[0], ahr, ah_s, ah_r)

        def new_state(y):
            third = rz[pl.ds(y, Z, stride=Y), :].T
            state = init[pl.ds(y, X, stride=Y), :] + third
            advy[y] = state
            lz[y] = lz[y] + (third - sec[y]) * (1.0 / HALF)
            adv[pl.ds(y, X, stride=Y), :] = state
        new_state(0)
        new_state(Y - 1)
        start_pair(a_up, a_down)
        for y in range(1, Y - 1):
            new_state(y)

        def y_op(s):
            cs = [cy[y, rows(s), :] for y in range(Y)]
            vs = [advy[y, rows(s), :] for y in range(Y)]
            fl = [0.5 * (cs[i] + cs[i + 1]) * (vs[i + 1] - vs[i]) for i in range(Y - 1)]
            for y in range(Y):
                out = lz[y, rows(s), :]
                if y < Y - 1:
                    out = out + fl[y]
                if y > 0:
                    out = out - fl[y - 1]
                upc[strided(s, y), :] = out
        loop(W, y_op, 4)

        loads[3].wait()

        def x_op(g):
            out = line_op(cond, adv, g, XB, zero, zero, zero, zero)
            for i in range(CELLS):
                j = g * CELLS + i
                put(upc, j, row(upc, j) + (row(heat, j) + out[i]))
        loop(XB, x_op, 2)

        recv_pair(a_up, a_down)

        def y_ends(s):
            for slot, y in ((0, 0), (1, Y - 1)):
                fl = 0.5 * (chr_[slot, rows(s), :] + cy[y, rows(s), :]) * (ahr[slot, rows(s), :] - advy[y, rows(s), :])
                upc[strided(s, y), :] = upc[strided(s, y), :] + fl
        loop(W, y_ends, 4)

        sent_pair(c_up, c_down)
        sent_pair(a_up, a_down)
        left(msend, mrecv, ms_s, ms_r, one)
        to_mate.wait_send()
        flux_mate.wait_send()

        @pl.when(skip_sends)
        def _():
            skip.wait_send()
        left(fs, frecv, fs_s, fs_r, two)
        z_left(zmat, zm_s, zm_r)
        z_left(zrhs, zr_s, zr_r)

    flat = pltpu.VMEM((X * Y, Z), F32)
    planes = pltpu.VMEM((Y, X, Z), F32)
    flux = lambda count: pltpu.VMEM((count, Y, Z), F32)
    part = lambda *lead: pltpu.VMEM((*lead, R, Z), F32)
    half = lambda *lead: pltpu.VMEM((*lead, H, Z), F32)
    sems = lambda count: pltpu.SemaphoreType.DMA((count,))
    scratch = [flat, flat, flat, flat, flat, flat, flat, flux(XB + 1), flat,
               planes, planes, planes, planes, planes, planes, planes,
               pltpu.VMEM((7, X, Z), F32), pltpu.VMEM((7, H, Z), F32), half(), half(), half(),
               part(C, 5), part(C, 5), part(C), part(C), part(C + 1), part(C, 2), half(2), half(2),
               flat, flat, flat, flat, flat, flat, flat, flat,
               flux(ZB + 1), flux(ZB + 1), flux(ZB + 1), flux(ZB), flux(ZB),
               pltpu.VMEM((N, 7, Y, Z), F32), pltpu.VMEM((N, 2, Y, Z), F32), flux(N + 1), planes, planes,
               half(), pltpu.VMEM((2, X, Z), F32), pltpu.VMEM((2, X, Z), F32),
               sems(C), sems(C), sems(C), sems(C), sems(1), sems(1), sems(1), sems(1), sems(1), sems(1), sems(N), sems(N), sems(N), sems(N),
               sems(2), sems(2), sems(2), sems(2), sems(4)]
    return kernel, scratch


def solution(mesh):
    W, N = mesh.shape["wide"], mesh.shape["narrow"]

    def per_device(*arrays):
        X, Y, Z = arrays[0].shape
        kernel, scratch = make_kernel(W, N, X, Y, Z)
        vmem = pl.BlockSpec(memory_space=pltpu.VMEM)
        out = pltpu.VMEM((X * Y, Z), F32)
        results = pl.pallas_call(
            kernel,
            out_shape=(out, out),
            in_specs=[pl.BlockSpec(memory_space=pltpu.HBM)] * 4,
            out_specs=(vmem, vmem),
            scratch_shapes=scratch,
            compiler_params=pltpu.CompilerParams(
                collective_id=0, has_side_effects=True, vmem_limit_bytes=54 * 1024 * 1024),
        )(*[a.reshape(X * Y, Z) for a in arrays])
        return tuple(r.reshape(X, Y, Z) for r in results)

    placed = P(None, "wide", "narrow")
    return jax.shard_map(
        per_device, mesh=mesh, in_specs=(placed,) * 4, out_specs=(placed, placed), check_vma=False)
```
